1024 devices in a mesh: rep: 32 (over z, x_hi), fsdp: 32 (over x_lo, y, core).
Axes of the slice: x: 8 (x_hi: 4, x_lo: 2; x = x_hi * 2 + x_lo), y: 8, z: 8, core: 2. Of those that a mesh axis runs over, the one named last changes fastest.
Arguments:
- attn_out: bfloat16 [16384, 4096], P(('rep', 'fsdp')), may hold values from -6 to 6
- residual: bfloat16 [16384, 8192], P('rep', 'fsdp')
- out_weight: bfloat16 [4096, 8192], P(None, 'fsdp'), may hold values from -0.09375 to 0.09375
- tangent: bfloat16 [4096, 8192], P(None, 'fsdp'), may hold values from -0.09375 to 0.09375
- norm_gain: bfloat16 [8192], P('fsdp'), may hold values from 0.5 to 1.5
- cotangent: bfloat16 [16384, 8192], P('rep', 'fsdp'), may hold values from -6 to 6
- seq_len: int32 [32], P('rep'), may hold values from 256 to 512, as said below
Outputs:
- hvp: bfloat16 [4096, 8192], P('rep', 'fsdp')
The draws below stay inside these ranges and needn't reach their ends.
Inputs may be any that keep to these rules, and one draw needn't show every extreme that they name: `seq_len`: every value lies in 256 to 512, and some group has exactly 512.
All inputs are finite; a program needn't handle non-finite values.
Results may differ from the reference program's by a relative error of at most 0.02.
Values may be sent and summed in bfloat16 or wider, within the bound.
No kernel may reach another device: no remote copies, remote signals or barrier semaphores. Data moves between devices by JAX's collectives and lax.ppermute only.
A program may use at most 32 MiB of HBM per device.

```python
import jax
import jax.numpy as jnp
from jax import lax

D = 8192
TG = 512
HQD = 4096
GROUPS = 32
TOKENS = 16384


def draw_residual(key, part):
    key_base = jax.random.fold_in(key, 11)
    key_rows = jax.random.fold_in(key, 12)
    base = jax.random.normal(key_base, (TOKENS, D), jnp.float32)
    row_scale = 10.0 ** jax.random.uniform(key_rows, (TOKENS, 1), jnp.float32, 0.0, 1.0)
    col_scale = 10.0 ** (jnp.arange(D, dtype=jnp.float32) / D)
    return (0.1 * base * row_scale * col_scale[None, :]).astype(jnp.bfloat16)


def draw_seq_len(key, part):
    key_len = jax.random.fold_in(key, 21)
    key_pick = jax.random.fold_in(key, 22)
    lengths = jax.random.randint(key_len, (GROUPS,), TG // 2, TG + 1).astype(jnp.int32)
    chosen = jax.random.randint(key_pick, (), 0, GROUPS)
    return lengths.at[chosen].set(TG).astype(jnp.int32)


def steps_of(own_key, dims, split, least, largest):
    def one(dim, blocks):
        heights = jax.random.uniform(jax.random.fold_in(jax.random.fold_in(own_key, 6), dim), (blocks,), jnp.float32, least / len(split), largest / len(split))
        return jnp.repeat(jnp.exp(heights), dims[dim] // blocks).reshape((-1,) + (1,) * (len(dims) - dim - 1))

    level = one(*split[0])
    for cut in split[1:]:
        level = level * one(*cut)
    return level


def centred(own_key, extent, deviation, bound, cuts=(), kind=jnp.bfloat16):
    values = jax.random.normal(own_key, extent, jnp.float32) * deviation
    if len(cuts) > 0:
        values = steps_of(own_key, extent, cuts, -0.22, 0.18) * values
    return jnp.clip(values, min=-bound, max=bound).astype(kind)


def setup_inputs(seed: int = 0) -> dict:
    streams_of = jax.random.split(jax.random.key(seed), 8)
    attn_out = centred(streams_of[0], (TOKENS, HQD), 1.0, 6.0, ((0, 1024),))
    residual = draw_residual(jax.random.fold_in(streams_of[7], 71), 0)
    out_weight = centred(streams_of[2], (HQD, D), HQD ** -0.5, 0.09375, ((1, 32),))
    tangent = centred(streams_of[3], (HQD, D), HQD ** -0.5, 0.09375, ((1, 32),))
    norm_gain = jnp.clip(1.0 + 0.1 * jax.random.normal(streams_of[4], (D,), jnp.float32), 0.5, 1.5).astype(jnp.bfloat16)
    cotangent = centred(streams_of[5], (TOKENS, D), 1.0, 6.0, ((0, 32), (1, 32)))
    seq_len = draw_seq_len(jax.random.fold_in(streams_of[7], 71), 0)
    return dict(attn_out=attn_out, residual=residual, out_weight=out_weight, tangent=tangent, norm_gain=norm_gain, cotangent=cotangent, seq_len=seq_len)


EPS = 1e-05

def second_order(stream, moved, weighted, sum_sq, along_c, tangent_c, cross):
    inv = lax.rsqrt(sum_sq / D + EPS)
    inv3 = inv * inv * inv
    inv5 = inv3 * inv * inv
    share = cross / D
    curv = -inv3 * share * weighted + 3.0 * inv5 * share * along_c * stream / D
    curv = curv - inv3 * tangent_c * stream / D - inv3 * along_c * moved / D
    return curv.astype(jnp.bfloat16)

def reference(attn_out, residual, out_weight, tangent, norm_gain, cotangent, seq_len):
    feats = attn_out.reshape(GROUPS, TG, HQD)
    resid_groups = residual.reshape(GROUPS, TG, D)
    cot_groups = cotangent.reshape(GROUPS, TG, D)
    gain = norm_gain.astype(jnp.float32)[None, :]

    def one_group(total, item):
        feat, resid_g, cot_g, length = item
        stream = resid_g.astype(jnp.float32) + jnp.dot(feat, out_weight, preferred_element_type=jnp.float32)
        moved = jnp.dot(feat, tangent, preferred_element_type=jnp.float32)
        live_rows = (jnp.arange(TG, dtype=jnp.int32) < length).astype(jnp.float32)[:, None]
        weighted = cot_g.astype(jnp.float32) * gain * live_rows
        sum_sq = lax.optimization_barrier(jnp.sum(stream * stream, axis=1, keepdims=True))
        along_c = lax.optimization_barrier(jnp.sum(weighted * stream, axis=1, keepdims=True))
        tangent_c = lax.optimization_barrier(jnp.sum(weighted * moved, axis=1, keepdims=True))
        cross = lax.optimization_barrier(jnp.sum(stream * moved, axis=1, keepdims=True))
        curv = second_order(stream, moved, weighted, sum_sq, along_c, tangent_c, cross)
        part = lax.dot_general(feat, curv, (((0,), (0,)), ((), ())), preferred_element_type=jnp.float32)
        part = lax.optimization_barrier(part.astype(jnp.bfloat16))
        return (total + part.astype(jnp.float32), None)
    start = jnp.zeros((HQD, D), jnp.float32)
    total, unused = lax.scan(one_group, start, (feats, resid_groups, cot_groups, seq_len))
    return total.astype(jnp.bfloat16)
```

```python
import jax
import jax.numpy as jnp
from jax import lax
from jax.experimental import pallas as pl
from jax.experimental.pallas import tpu as pltpu
from jax.sharding import PartitionSpec as P

D = 8192
EPS = 1e-05
NX, NY, NC = 2, 8, 2
NZ, NH = 8, 4
SHARD = 16
VMEM = pl.BlockSpec(memory_space=pltpu.VMEM)
SMEM = pl.BlockSpec(memory_space=pltpu.SMEM)
ANY = pl.BlockSpec(memory_space=pl.ANY)
PARAMS = pltpu.CompilerParams(vmem_limit_bytes=48 * 1024 * 1024)


def fsdp_perm(dx, dy, dc):
    moves = []
    for x in range(NX):
        for y in range(NY):
            for c in range(NC):
                there = (((x + dx) % NX) * NY + (y + dy) % NY) * NC + (c + dc) % NC
                moves.append(((x * NY + y) * NC + c, there))
    return moves


def rep_perm(dz, dh):
    return [
        (z * NH + h, ((z + dz) % NZ) * NH + (h + dh) % NH)
        for z in range(NZ)
        for h in range(NH)
    ]


CLASSES = [
    [z * NH + h for z in range(NZ) for h in range(NH) if (z + 2 * h) % 4 == c]
    for c in range(4)
]


def token_blocks(me, other_core):
    x, y, c = me // (NY * NC), (me // NC) % NY, me % NC
    c = 1 - c if other_core else c
    blocks = []
    for gx, gy in ((0, 0), (0, -1), (0, 1), (1, 0)):
        for sx, sy in ((0, 0), (0, 4), (1, -2), (1, 2)):
            cx = (x + gx + sx) % NX
            cy = (y + gy + sy + NY) % NY
            blocks.append((cx * NY + cy) * NC + c)
    return blocks


def rows_of(block):
    return pl.ds(pl.multiple_of(block * SHARD, SHARD), SHARD)


def weighted_of(cot_ref, gain_ref, length, rows, first):
    token = first + lax.broadcasted_iota(jnp.int32, (rows, 1), 0)
    live = (token < length).astype(jnp.float32)
    return (
        cot_ref[pl.ds(first, rows), :].astype(jnp.float32)
        * gain_ref[...].astype(jnp.float32)
        * live
    )


def first_kernel(me_ref, len_ref, *refs):
    pieces = refs[:8]
    w_ref, t_ref, res_ref, cot_ref, gain_ref = refs[8:13]
    a_ref, stream_ref, moved_ref, stats_ref, sems = refs[13:]
    rows = a_ref.shape[0]
    part = rows // 8
    copies = [
        pltpu.make_async_copy(piece, a_ref.at[pl.ds(i * part, part)], sems.at[i])
        for i, piece in enumerate(pieces)
    ]
    for copy in copies:
        copy.start()
    me = me_ref[0]
    for half in range(2):
        for copy in copies[4 * half : 4 * half + 4]:
            copy.wait()
        a = a_ref[pl.ds(half * 4 * part, 4 * part), :]
        s = jnp.dot(a, w_ref[...], preferred_element_type=jnp.float32)
        m = jnp.dot(a, t_ref[...], preferred_element_type=jnp.float32)
        for i, block in enumerate(token_blocks(me, half == 1)):
            stream_ref[rows_of(block), :] = s[i * SHARD : (i + 1) * SHARD]
            moved_ref[rows_of(block), :] = m[i * SHARD : (i + 1) * SHARD]
    stream = stream_ref[...] + res_ref[...].astype(jnp.float32)
    stream_ref[...] = stream
    moved = moved_ref[...]
    weighted = weighted_of(cot_ref, gain_ref, len_ref[0], rows, 0)
    sums = [
        jnp.sum(stream * stream, axis=1, keepdims=True),
        jnp.sum(weighted * stream, axis=1, keepdims=True),
        jnp.sum(weighted * moved, axis=1, keepdims=True),
        jnp.sum(stream * moved, axis=1, keepdims=True),
    ]
    lane = lax.broadcasted_iota(jnp.int32, (rows, 128), 1)
    table = jnp.zeros((rows, 128), jnp.float32)
    for i, value in enumerate(sums):
        table = jnp.where(lane == i, value, table)
    turned = table.T
    half = rows // 2
    packed = jnp.concatenate([turned[:4, :half], turned[:4, half:]], axis=0)
    for i in range(stats_ref.shape[0]):
        stats_ref[i] = packed


def second_kernel(
    ids_ref, len_ref, stats_ref, stream_ref, moved_ref, cot_ref, gain_ref, a_ref,
    own_ref, up_ref, down_ref, right_ref, left_ref, curv_ref,
):
    total = jnp.sum(stats_ref[...], axis=0)
    half = total.shape[1]
    coefs = []
    for h in range(2):
        sum_sq, along_c, tangent_c, cross = (
            total[4 * h + i : 4 * h + i + 1] for i in range(4)
        )
        inv = lax.rsqrt(sum_sq / D + EPS)
        inv3 = inv * inv * inv
        inv5 = inv3 * inv * inv
        share = cross / D
        coefs.append(-inv3 * share)
        coefs.append((3.0 * inv5 * share * along_c - inv3 * tangent_c) / D)
        coefs.append(-inv3 * along_c / D)
    coefs.append(jnp.zeros((128 - len(coefs), half), jnp.float32))
    turned = jnp.concatenate(coefs, axis=0).T
    for h in range(2):
        rows = pl.ds(h * half, half)
        weighted = weighted_of(cot_ref, gain_ref, len_ref[0], half, h * half)
        curv_ref[rows, :] = (
            turned[:, 3 * h : 3 * h + 1] * weighted
            + turned[:, 3 * h + 1 : 3 * h + 2] * stream_ref[rows, :]
            + turned[:, 3 * h + 2 : 3 * h + 3] * moved_ref[rows, :]
        )
    me = ids_ref[0]
    blocks = token_blocks(me, False) + token_blocks(me, True)
    curv = jnp.concatenate([curv_ref[rows_of(b), :] for b in blocks], axis=0)
    curv_t = curv.T.astype(jnp.bfloat16)
    color = ids_ref[1]
    for r in (1, 3, 2, 0):
        c = (color + r) % 4
        for pair in range(4):
            z = 2 * pair + c % 2
            h = ((z - c + 8) % 4) // 2
            columns = [
                a_ref[:, pl.ds(pl.multiple_of((z * NH + h + 2 * k) * 128, 128), 128)]
                for k in range(2)
            ]
            out = jnp.dot(
                curv_t,
                jnp.concatenate(columns, axis=1),
                preferred_element_type=jnp.float32,
            ).astype(jnp.bfloat16)
            for k in range(2):
                i = 2 * pair + k
                value = out[:, 128 * k : 128 * k + 128]
                if r == 0:
                    own_ref[i] = value
                elif r == 1:
                    up_ref[i] = value
                elif r == 3:
                    down_ref[i] = value
                elif i < 4:
                    right_ref[i] = value
                else:
                    left_ref[i - 4] = value


def third_kernel(own_ref, below_ref, above_ref, left_ref, right_ref, out_ref):
    f32 = jnp.float32
    for i in range(8):
        side = left_ref[i] if i < 4 else right_ref[i - 4]
        out_ref[i] = (
            own_ref[i].astype(f32)
            + below_ref[i].astype(f32)
            + above_ref[i].astype(f32)
            + side.astype(f32)
        ).astype(out_ref.dtype)


def last_kernel(parts_ref, out_ref):
    total = parts_ref[0].astype(jnp.float32)
    for i in range(1, parts_ref.shape[0]):
        total = total + parts_ref[i].astype(jnp.float32)
    out_ref[...] = total.T.astype(out_ref.dtype)


def local(attn_out, residual, out_weight, tangent, norm_gain, cotangent, seq_len):
    f32, bf16 = jnp.float32, jnp.bfloat16
    rows, columns = residual.shape
    features = attn_out.shape[1]
    me = lax.axis_index("fsdp")
    rep = lax.axis_index("rep")
    color = (rep // NH + 2 * (rep % NH)) % 4
    ids = jnp.stack([me, color]).astype(jnp.int32)
    gain = norm_gain[None, :]

    def send(x, *step):
        return lax.ppermute(x, "fsdp", fsdp_perm(*step))

    own = jnp.concatenate(
        [
            attn_out,
            send(attn_out, 0, 4, 0),
            send(attn_out, 1, 2, 0),
            send(attn_out, 1, -2, 0),
        ],
        axis=0,
    )
    near = [own, send(own, 0, 1, 0), send(own, 0, -1, 0), send(own, 1, 0, 0)]
    far = [send(x, 0, 0, 1) for x in near]

    a, stream, moved, stats = pl.pallas_call(
        first_kernel,
        out_shape=(
            jax.ShapeDtypeStruct((rows, features), bf16),
            jax.ShapeDtypeStruct((rows, columns), f32),
            jax.ShapeDtypeStruct((rows, columns), f32),
            jax.ShapeDtypeStruct((32, 8, rows // 2), f32),
        ),
        in_specs=[SMEM, SMEM] + [ANY] * 8 + [VMEM] * 5,
        out_specs=(VMEM,) * 4,
        scratch_shapes=[pltpu.SemaphoreType.DMA((8,))],
        compiler_params=PARAMS,
        name="first",
    )(ids, seq_len, *near, *far, out_weight, tangent, residual, cotangent, gain)

    stats = lax.all_to_all(stats, "fsdp", 0, 0)

    whole = jax.ShapeDtypeStruct((8, columns, 128), bf16)
    part = jax.ShapeDtypeStruct((4, columns, 128), bf16)
    mine, up, down, right, left = pl.pallas_call(
        second_kernel,
        out_shape=(whole, whole, whole, part, part),
        in_specs=[SMEM, SMEM] + [VMEM] * 6,
        out_specs=(VMEM,) * 5,
        scratch_shapes=[pltpu.VMEM((rows, columns), f32)],
        compiler_params=PARAMS,
        name="second",
    )(ids, seq_len, stats, stream, moved, cotangent, gain, a)

    below = lax.ppermute(up, "rep", rep_perm(1, 0))
    above = lax.ppermute(down, "rep", rep_perm(-1, 0))
    from_left = lax.ppermute(right, "rep", rep_perm(0, 1))
    from_right = lax.ppermute(left, "rep", rep_perm(0, -1))
    four = pl.pallas_call(
        third_kernel,
        out_shape=whole,
        in_specs=[VMEM] * 5,
        out_specs=VMEM,
        compiler_params=PARAMS,
        name="third",
    )(mine, below, above, from_left, from_right)
    parts = lax.all_to_all(four, "rep", 0, 0, axis_index_groups=CLASSES)
    return pl.pallas_call(
        last_kernel,
        out_shape=jax.ShapeDtypeStruct((128, columns), bf16),
        in_specs=[VMEM],
        out_specs=VMEM,
        compiler_params=PARAMS,
        name="last",
    )(parts)


def solution(mesh):
    in_specs = (
        P(("rep", "fsdp"), None),
        P("rep", "fsdp"),
        P(None, "fsdp"),
        P(None, "fsdp"),
        P("fsdp"),
        P("rep", "fsdp"),
        P("rep"),
    )
    out_specs = P("rep", "fsdp")
    return jax.shard_map(local, mesh=mesh, in_specs=in_specs, out_specs=out_specs, check_vma=False)
```

```python
import jax
import jax.numpy as jnp
from jax import lax
from jax.experimental import pallas as pl
from jax.experimental.pallas import tpu as pltpu
from jax.sharding import PartitionSpec as P

D = 8192
EPS = 1e-05
NX, NY, NC = 2, 8, 2
NZ, NH = 8, 4
SHARD = 16
PIECE = 64
HALF = 256
VMEM = pl.BlockSpec(memory_space=pltpu.VMEM)
SMEM = pl.BlockSpec(memory_space=pltpu.SMEM)
ANY = pl.BlockSpec(memory_space=pl.ANY)
PARAMS = pltpu.CompilerParams(vmem_limit_bytes=16 * 1024 * 1024)


def fsdp_of(x, y, c):
    return (x % NX * NY + y % NY) * NC + c % NC


def fsdp_perm(step):
    return [
        (fsdp_of(x, y, c), fsdp_of(*step(x, y, c)))
        for x in range(NX)
        for y in range(NY)
        for c in range(NC)
    ]


def rep_of(z, h):
    return z % NZ * NH + h % NH


def rep_perm(step):
    return [(rep_of(z, h), rep_of(*step(z, h))) for z in range(NZ) for h in range(NH)]


def even_partner(i):
    return i ^ 1


def odd_partner(i):
    return ((i + 1) ^ 1) - 1


def chip_of(q, j):
    x = j // 2
    return x, (q + 2 * x) % 4 + 4 * (j % 2)


TEAMS = [[fsdp_of(*chip_of(q, j), c) for j in range(4)] for q in range(4) for c in range(NC)]
CLASSES = [
    [rep_of(z, h) for z in range(NZ) for h in range(NH) if (z + 2 * h) % 4 == q]
    for q in range(4)
]
BLOCKS = [fsdp_of(*chip_of(q, j), c) for c in range(NC) for q in range(4) for j in range(4)]


def piece_colors(me):
    x, y = me // (NY * NC), (me // NC) % NY
    own = (y + 2 * x) % 4
    to_even = 1 + 2 * (y % 2)
    return [own, (own + to_even) % 4, (own + 4 - to_even) % 4, (own + 2) % 4]


def piece_rows(first, color):
    return pl.ds(pl.multiple_of(first + color * PIECE, PIECE), PIECE)


def prep_kernel(len_ref, after_ref, res_ref, cot_ref, gain_ref, res_out, weighted_ref):
    gain = gain_ref[...].astype(jnp.float32)
    for i, block in enumerate(BLOCKS):
        token = block * SHARD + lax.broadcasted_iota(jnp.int32, (SHARD, 1), 0)
        live = (token < len_ref[0]).astype(jnp.float32)
        there = pl.ds(i * SHARD, SHARD)
        here = pl.ds(block * SHARD, SHARD)
        weighted_ref[there, :] = cot_ref[here, :].astype(jnp.float32) * gain * live
        res_out[there, :] = res_ref[here, :].astype(jnp.float32)


def products(pieces, w_ref, t_ref):
    a = jnp.concatenate([piece[...] for piece in pieces], axis=0)
    return (
        jnp.dot(a, w_ref[...], preferred_element_type=jnp.float32),
        jnp.dot(a, t_ref[...], preferred_element_type=jnp.float32),
    )


def near_kernel(p0, p1, p2, p3, w_ref, t_ref, s_ref, m_ref):
    s_ref[...], m_ref[...] = products((p0, p1, p2, p3), w_ref, t_ref)


def far_kernel(
    me_ref, p0, p1, p2, p3, w_ref, t_ref, near_s_ref, near_m_ref, res_ref, weighted_ref,
    stream_ref, moved_ref, stats_ref,
):
    me = me_ref[0]
    core = me % NC
    s, m = products((p0, p1, p2, p3), w_ref, t_ref)
    for i, color in enumerate(piece_colors(me)):
        here = slice(i * PIECE, (i + 1) * PIECE)
        near = piece_rows(core * HALF, color)
        far = piece_rows((1 - core) * HALF, color)
        stream_ref[near, :] = near_s_ref[here, :]
        moved_ref[near, :] = near_m_ref[here, :]
        stream_ref[far, :] = s[here]
        moved_ref[far, :] = m[here]
    stream = stream_ref[...] + res_ref[...]
    stream_ref[...] = stream
    moved = moved_ref[...]
    weighted = weighted_ref[...]
    sums = [
        jnp.sum(stream * stream, axis=1, keepdims=True),
        jnp.sum(weighted * stream, axis=1, keepdims=True),
        jnp.sum(weighted * moved, axis=1, keepdims=True),
        jnp.sum(stream * moved, axis=1, keepdims=True),
    ]
    lane = lax.broadcasted_iota(jnp.int32, (2 * HALF, 128), 1)
    table = jnp.zeros((2 * HALF, 128), jnp.float32)
    for i, value in enumerate(sums):
        table = jnp.where(lane == i, value, table)
    turned = table.T
    packed = jnp.concatenate([turned[:4, :HALF], turned[:4, HALF:]], axis=0)
    for i in range(stats_ref.shape[0]):
        stats_ref[i] = packed


def second_kernel(
    ids_ref, stats_ref, stream_ref, moved_ref, weighted_ref,
    n0, n1, n2, n3, f0, f1, f2, f3,
    own_ref, even_ref, odd_ref, first_ref, later_ref, curv_ref,
):
    total = jnp.sum(stats_ref[...], axis=0)
    coefs = []
    for h in range(2):
        sum_sq, along_c, tangent_c, cross = (
            total[4 * h + i : 4 * h + i + 1] for i in range(4)
        )
        inv = lax.rsqrt(sum_sq / D + EPS)
        inv3 = inv * inv * inv
        inv5 = inv3 * inv * inv
        share = cross / D
        coefs.append(-inv3 * share)
        coefs.append((3.0 * inv5 * share * along_c - inv3 * tangent_c) / D)
        coefs.append(-inv3 * along_c / D)
    coefs.append(jnp.zeros((128 - len(coefs), HALF), jnp.float32))
    turned = jnp.concatenate(coefs, axis=0).T
    for h in range(2):
        rows = pl.ds(h * HALF, HALF)
        curv_ref[rows, :] = (
            turned[:, 3 * h : 3 * h + 1] * weighted_ref[rows, :]
            + turned[:, 3 * h + 1 : 3 * h + 2] * stream_ref[rows, :]
            + turned[:, 3 * h + 2 : 3 * h + 3] * moved_ref[rows, :]
        )
    me = ids_ref[0]
    core = me % NC
    colors = piece_colors(me)
    curv = jnp.concatenate(
        [curv_ref[piece_rows(core * HALF, q), :] for q in colors]
        + [curv_ref[piece_rows((1 - core) * HALF, q), :] for q in colors],
        axis=0,
    )
    curv_t = curv.T.astype(jnp.bfloat16)
    pieces = (n0, n1, n2, n3, f0, f1, f2, f3)
    color = ids_ref[1]
    to_even = 1 + 2 * (color % 2)
    for what, step in (("even", to_even), ("odd", 4 - to_even), ("side", 2), ("own", 0)):
        q = (color + step) % 4
        for pair in range(4):
            z = 2 * pair + q % 2
            h = ((z - q + 8) % 4) // 2
            columns = []
            for k in range(2):
                at = pl.ds(pl.multiple_of((z * NH + h + 2 * k) * 128, 128), 128)
                columns.append(jnp.concatenate([p[:, at] for p in pieces], axis=0))
            out = jnp.dot(
                curv_t,
                jnp.concatenate(columns, axis=1),
                preferred_element_type=jnp.float32,
            ).astype(jnp.bfloat16)
            for k in range(2):
                i = 2 * pair + k
                value = out[:, 128 * k : 128 * k + 128]
                if what == "own":
                    own_ref[i] = value
                elif what == "even":
                    even_ref[i] = value
                elif what == "odd":
                    odd_ref[i] = value
                elif i < 4:
                    first_ref[i] = value
                else:
                    later_ref[i - 4] = value


def third_kernel(own_ref, even_ref, odd_ref, first_ref, later_ref, out_ref):
    f32 = jnp.float32
    for i in range(8):
        side = first_ref[i] if i < 4 else later_ref[i - 4]
        out_ref[i] = (
            own_ref[i].astype(f32)
            + even_ref[i].astype(f32)
            + odd_ref[i].astype(f32)
            + side.astype(f32)
        ).astype(out_ref.dtype)


def last_kernel(parts_ref, out_ref):
    total = parts_ref[0].astype(jnp.float32)
    for i in range(1, parts_ref.shape[0]):
        total = total + parts_ref[i].astype(jnp.float32)
    out_ref[...] = total.T.astype(out_ref.dtype)


def local(attn_out, residual, out_weight, tangent, norm_gain, cotangent, seq_len):
    f32, bf16 = jnp.float32, jnp.bfloat16
    rows, columns = residual.shape
    features = attn_out.shape[1]
    me = lax.axis_index("fsdp")
    rep = lax.axis_index("rep")
    color = (rep // NH + 2 * (rep % NH)) % 4
    ids = jnp.stack([me, color]).astype(jnp.int32)
    gain = norm_gain[None, :]

    def in_group(x, step):
        return lax.ppermute(x, "fsdp", fsdp_perm(step))

    def of_groups(x, step):
        return lax.ppermute(x, "rep", rep_perm(step))

    def shape(*dims, dtype=f32):
        return jax.ShapeDtypeStruct(dims, dtype)

    own = lax.all_to_all(
        jnp.broadcast_to(attn_out[None], (4, SHARD, features)),
        "fsdp", 0, 0, axis_index_groups=TEAMS,
    ).reshape(PIECE, features)
    near = [
        own,
        in_group(own, lambda x, y, c: (x, even_partner(y), c)),
        in_group(own, lambda x, y, c: (x, odd_partner(y), c)),
        in_group(own, lambda x, y, c: (x + 1, y, c)),
    ]
    res, weighted = pl.pallas_call(
        prep_kernel,
        out_shape=(shape(rows, columns), shape(rows, columns)),
        in_specs=[SMEM, ANY, VMEM, VMEM, VMEM],
        out_specs=(VMEM,) * 2,
        compiler_params=PARAMS,
        name="prep",
    )(seq_len, own, residual, cotangent, gain)
    near[3], res = lax.optimization_barrier((near[3], res))

    far = [in_group(piece, lambda x, y, c: (x, y, c + 1)) for piece in near]

    near_s, near_m = pl.pallas_call(
        near_kernel,
        out_shape=(shape(HALF, columns), shape(HALF, columns)),
        in_specs=[VMEM] * 6,
        out_specs=(VMEM,) * 2,
        compiler_params=PARAMS,
        name="near",
    )(*near, out_weight, tangent)

    stream, moved, stats = pl.pallas_call(
        far_kernel,
        out_shape=(shape(rows, columns), shape(rows, columns), shape(32, 8, HALF)),
        in_specs=[SMEM] + [VMEM] * 10,
        out_specs=(VMEM,) * 3,
        compiler_params=PARAMS,
        name="far",
    )(ids, *far, out_weight, tangent, near_s, near_m, res, weighted)

    stats = lax.all_to_all(stats, "fsdp", 0, 0)

    whole = shape(8, columns, 128, dtype=bf16)
    part = shape(4, columns, 128, dtype=bf16)
    mine, even, odd, first, later = pl.pallas_call(
        second_kernel,
        out_shape=(whole, whole, whole, part, part),
        in_specs=[SMEM] + [VMEM] * 12,
        out_specs=(VMEM,) * 5,
        scratch_shapes=[pltpu.VMEM((rows, columns), f32)],
        compiler_params=PARAMS,
        name="second",
    )(ids, stats, stream, moved, weighted, *near, *far)

    even = of_groups(even, lambda z, h: (even_partner(z), h))
    odd = of_groups(odd, lambda z, h: (odd_partner(z), h))
    first = of_groups(first, lambda z, h: (z, even_partner(h)))
    later = of_groups(later, lambda z, h: (z, odd_partner(h)))
    four = pl.pallas_call(
        third_kernel,
        out_shape=whole,
        in_specs=[VMEM] * 5,
        out_specs=VMEM,
        compiler_params=PARAMS,
        name="third",
    )(mine, even, odd, first, later)
    parts = lax.all_to_all(four, "rep", 0, 0, axis_index_groups=CLASSES)
    return pl.pallas_call(
        last_kernel,
        out_shape=shape(128, columns, dtype=bf16),
        in_specs=[VMEM],
        out_specs=VMEM,
        compiler_params=PARAMS,
        name="last",
    )(parts)


def solution(mesh):
    in_specs = (
        P(("rep", "fsdp"), None),
        P("rep", "fsdp"),
        P(None, "fsdp"),
        P(None, "fsdp"),
        P("fsdp"),
        P("rep", "fsdp"),
        P("rep"),
    )
    out_specs = P("rep", "fsdp")
    return jax.shard_map(local, mesh=mesh, in_specs=in_specs, out_specs=out_specs, check_vma=False)
```

```python
import jax
import jax.numpy as jnp
from jax import lax
from jax.experimental import pallas as pl
from jax.experimental.pallas import tpu as pltpu
from jax.sharding import PartitionSpec as P

D = 8192
EPS = 1e-05
NX, NY, NC = 2, 8, 2
NZ, NH = 8, 4
SHARD = 16
PIECE = 64
HALF = 256
VMEM = pl.BlockSpec(memory_space=pltpu.VMEM)
SMEM = pl.BlockSpec(memory_space=pltpu.SMEM)
ANY = pl.BlockSpec(memory_space=pl.ANY)
PARAMS = pltpu.CompilerParams(vmem_limit_bytes=16 * 1024 * 1024)


def fsdp_of(x, y, c):
    return (x % NX * NY + y % NY) * NC + c % NC


def fsdp_perm(step):
    return [
        (fsdp_of(x, y, c), fsdp_of(*step(x, y, c)))
        for x in range(NX)
        for y in range(NY)
        for c in range(NC)
    ]


def rep_of(z, h):
    return z % NZ * NH + h % NH


def rep_perm(step):
    return [(rep_of(z, h), rep_of(*step(z, h))) for z in range(NZ) for h in range(NH)]


def even_partner(i):
    return i ^ 1


def odd_partner(i):
    return ((i + 1) ^ 1) - 1


def chip_of(q, j):
    x = j // 2
    return x, (q + 2 * x) % 4 + 4 * (j % 2)


TEAMS = [[fsdp_of(*chip_of(q, j), c) for j in range(4)] for q in range(4) for c in range(NC)]
CLASSES = [
    [rep_of(z, h) for z in range(NZ) for h in range(NH) if (z + 2 * h) % 4 == q]
    for q in range(4)
]
BLOCKS = [fsdp_of(*chip_of(q, j), c) for c in range(NC) for q in range(4) for j in range(4)]


def piece_colors(me):
    x, y = me // (NY * NC), (me // NC) % NY
    own = (y + 2 * x) % 4
    to_even = 1 + 2 * (y % 2)
    return [own, (own + to_even) % 4, (own + 4 - to_even) % 4, (own + 2) % 4]


def piece_rows(first, color):
    return pl.ds(pl.multiple_of(first + color * PIECE, PIECE), PIECE)


def prep_kernel(len_ref, after_ref, res_ref, cot_ref, gain_ref, res_out, weighted_ref):
    gain = gain_ref[...].astype(jnp.float32)
    for i, block in enumerate(BLOCKS):
        token = block * SHARD + lax.broadcasted_iota(jnp.int32, (SHARD, 1), 0)
        live = (token < len_ref[0]).astype(jnp.float32)
        there = pl.ds(i * SHARD, SHARD)
        here = pl.ds(block * SHARD, SHARD)
        weighted_ref[there, :] = cot_ref[here, :].astype(jnp.float32) * gain * live
        res_out[there, :] = res_ref[here, :].astype(jnp.float32)


def product(pieces, w_ref):
    a = jnp.concatenate([piece[...] for piece in pieces], axis=0)
    return jnp.dot(a, w_ref[...], preferred_element_type=jnp.float32)


def near_kernel(p0, p1, p2, p3, w_ref, s_ref):
    s_ref[...] = product((p0, p1, p2, p3), w_ref)


def far_kernel(
    me_ref, p0, p1, p2, p3, w_ref, t_ref, near_s_ref, near_m_ref, res_ref, weighted_ref,
    stream_ref, moved_ref, stats_ref,
):
    me = me_ref[0]
    core = me % NC
    pieces = (p0, p1, p2, p3)
    s, m = product(pieces, w_ref), product(pieces, t_ref)
    for i, color in enumerate(piece_colors(me)):
        here = slice(i * PIECE, (i + 1) * PIECE)
        near = piece_rows(core * HALF, color)
        far = piece_rows((1 - core) * HALF, color)
        stream_ref[near, :] = near_s_ref[here, :]
        moved_ref[near, :] = near_m_ref[here, :]
        stream_ref[far, :] = s[here]
        moved_ref[far, :] = m[here]
    stream = stream_ref[...] + res_ref[...]
    stream_ref[...] = stream
    moved = moved_ref[...]
    weighted = weighted_ref[...]
    sums = [
        jnp.sum(stream * stream, axis=1, keepdims=True),
        jnp.sum(weighted * stream, axis=1, keepdims=True),
        jnp.sum(weighted * moved, axis=1, keepdims=True),
        jnp.sum(stream * moved, axis=1, keepdims=True),
    ]
    lane = lax.broadcasted_iota(jnp.int32, (2 * HALF, 128), 1)
    table = jnp.zeros((2 * HALF, 128), jnp.float32)
    for i, value in enumerate(sums):
        table = jnp.where(lane == i, value, table)
    turned = table.T
    packed = jnp.concatenate([turned[:4, :HALF], turned[:4, HALF:]], axis=0)
    for i in range(stats_ref.shape[0]):
        stats_ref[i] = packed


def second_kernel(
    ids_ref, stats_ref, stream_ref, moved_ref, weighted_ref,
    n0, n1, n2, n3, f0, f1, f2, f3,
    own_ref, even_ref, odd_ref, first_ref, later_ref, curv_ref, a_ref, sems,
):
    copies = [
        pltpu.make_async_copy(piece, a_ref.at[pl.ds(i * PIECE, PIECE)], sems.at[i])
        for i, piece in enumerate((n0, n1, n2, n3, f0, f1, f2, f3))
    ]
    for copy in copies:
        copy.start()
    total = jnp.sum(stats_ref[...], axis=0)
    coefs = []
    for h in range(2):
        sum_sq, along_c, tangent_c, cross = (
            total[4 * h + i : 4 * h + i + 1] for i in range(4)
        )
        inv = lax.rsqrt(sum_sq / D + EPS)
        inv3 = inv * inv * inv
        inv5 = inv3 * inv * inv
        share = cross / D
        coefs.append(-inv3 * share)
        coefs.append((3.0 * inv5 * share * along_c - inv3 * tangent_c) / D)
        coefs.append(-inv3 * along_c / D)
    coefs.append(jnp.zeros((128 - len(coefs), HALF), jnp.float32))
    turned = jnp.concatenate(coefs, axis=0).T
    for h in range(2):
        rows = pl.ds(h * HALF, HALF)
        curv_ref[rows, :] = (
            turned[:, 3 * h : 3 * h + 1] * weighted_ref[rows, :]
            + turned[:, 3 * h + 1 : 3 * h + 2] * stream_ref[rows, :]
            + turned[:, 3 * h + 2 : 3 * h + 3] * moved_ref[rows, :]
        )
    me = ids_ref[0]
    core = me % NC
    colors = piece_colors(me)
    curv = jnp.concatenate(
        [curv_ref[piece_rows(core * HALF, q), :] for q in colors]
        + [curv_ref[piece_rows((1 - core) * HALF, q), :] for q in colors],
        axis=0,
    )
    curv_t = curv.T.astype(jnp.bfloat16)
    for copy in copies:
        copy.wait()
    color = ids_ref[1]
    to_even = 1 + 2 * (color % 2)
    for what, step in (("side", 2), ("even", to_even), ("odd", 4 - to_even), ("own", 0)):
        q = (color + step) % 4
        for pair in range(4):
            z = 2 * pair + q % 2
            h = ((z - q + 8) % 4) // 2
            columns = []
            for k in range(2):
                at = pl.ds(pl.multiple_of((z * NH + h + 2 * k) * 128, 128), 128)
                columns.append(a_ref[:, at])
            out = jnp.dot(
                curv_t,
                jnp.concatenate(columns, axis=1),
                preferred_element_type=jnp.float32,
            ).astype(jnp.bfloat16)
            for k in range(2):
                i = 2 * pair + k
                value = out[:, 128 * k : 128 * k + 128]
                if what == "own":
                    own_ref[i] = value
                elif what == "even":
                    even_ref[i] = value
                elif what == "odd":
                    odd_ref[i] = value
                elif i < 4:
                    first_ref[i] = value
                else:
                    later_ref[i - 4] = value


def third_kernel(own_ref, even_ref, odd_ref, first_ref, later_ref, out_ref):
    f32 = jnp.float32
    for i in range(8):
        side = first_ref[i] if i < 4 else later_ref[i - 4]
        out_ref[i] = (
            own_ref[i].astype(f32)
            + even_ref[i].astype(f32)
            + odd_ref[i].astype(f32)
            + side.astype(f32)
        ).astype(out_ref.dtype)


def last_kernel(parts_ref, out_ref):
    total = parts_ref[0].astype(jnp.float32)
    for i in range(1, parts_ref.shape[0]):
        total = total + parts_ref[i].astype(jnp.float32)
    out_ref[...] = total.T.astype(out_ref.dtype)


def local(attn_out, residual, out_weight, tangent, norm_gain, cotangent, seq_len):
    f32, bf16 = jnp.float32, jnp.bfloat16
    rows, columns = residual.shape
    features = attn_out.shape[1]
    me = lax.axis_index("fsdp")
    rep = lax.axis_index("rep")
    color = (rep // NH + 2 * (rep % NH)) % 4
    ids = jnp.stack([me, color]).astype(jnp.int32)
    gain = norm_gain[None, :]

    def in_group(x, step):
        return lax.ppermute(x, "fsdp", fsdp_perm(step))

    def of_groups(x, step):
        return lax.ppermute(x, "rep", rep_perm(step))

    def shape(*dims, dtype=f32):
        return jax.ShapeDtypeStruct(dims, dtype)

    own = lax.all_to_all(
        jnp.broadcast_to(attn_out[None], (4, SHARD, features)),
        "fsdp", 0, 0, axis_index_groups=TEAMS,
    ).reshape(PIECE, features)
    near = [
        own,
        in_group(own, lambda x, y, c: (x, even_partner(y), c)),
        in_group(own, lambda x, y, c: (x, odd_partner(y), c)),
        in_group(own, lambda x, y, c: (x + 1, y, c)),
    ]
    res, weighted = pl.pallas_call(
        prep_kernel,
        out_shape=(shape(rows, columns), shape(rows, columns)),
        in_specs=[SMEM, ANY, VMEM, VMEM, VMEM],
        out_specs=(VMEM,) * 2,
        compiler_params=PARAMS,
        name="prep",
    )(seq_len, own, residual, cotangent, gain)
    ready, res = lax.optimization_barrier((own, res))

    far = [in_group(piece, lambda x, y, c: (x, y, c + 1)) for piece in [ready] + near[1:]]

    near_s, near_m = (
        pl.pallas_call(
            near_kernel,
            out_shape=shape(HALF, columns),
            in_specs=[VMEM] * 5,
            out_specs=VMEM,
            compiler_params=PARAMS,
            name=name,
        )(*near, w)
        for name, w in (("near_s", out_weight), ("near_m", tangent))
    )

    stream, moved, stats = pl.pallas_call(
        far_kernel,
        out_shape=(shape(rows, columns), shape(rows, columns), shape(32, 8, HALF)),
        in_specs=[SMEM] + [VMEM] * 10,
        out_specs=(VMEM,) * 3,
        compiler_params=PARAMS,
        name="far",
    )(ids, *far, out_weight, tangent, near_s, near_m, res, weighted)

    stats = lax.all_to_all(stats, "fsdp", 0, 0)

    whole = shape(8, columns, 128, dtype=bf16)
    part = shape(4, columns, 128, dtype=bf16)
    mine, even, odd, first, later = pl.pallas_call(
        second_kernel,
        out_shape=(whole, whole, whole, part, part),
        in_specs=[SMEM] + [VMEM] * 4 + [ANY] * 8,
        out_specs=(VMEM,) * 5,
        scratch_shapes=[
            pltpu.VMEM((rows, columns), f32),
            pltpu.VMEM((rows, features), bf16),
            pltpu.SemaphoreType.DMA((8,)),
        ],
        compiler_params=PARAMS,
        name="second",
    )(ids, stats, stream, moved, weighted, *near, *far)

    first = of_groups(first, lambda z, h: (z, even_partner(h)))
    later = of_groups(later, lambda z, h: (z, odd_partner(h)))
    even = of_groups(even, lambda z, h: (even_partner(z), h))
    odd = of_groups(odd, lambda z, h: (odd_partner(z), h))
    four = pl.pallas_call(
        third_kernel,
        out_shape=whole,
        in_specs=[VMEM] * 5,
        out_specs=VMEM,
        compiler_params=PARAMS,
        name="third",
    )(mine, even, odd, first, later)
    parts = lax.all_to_all(four, "rep", 0, 0, axis_index_groups=CLASSES)
    return pl.pallas_call(
        last_kernel,
        out_shape=shape(128, columns, dtype=bf16),
        in_specs=[VMEM],
        out_specs=VMEM,
        compiler_params=PARAMS,
        name="last",
    )(parts)


def solution(mesh):
    in_specs = (
        P(("rep", "fsdp"), None),
        P("rep", "fsdp"),
        P(None, "fsdp"),
        P(None, "fsdp"),
        P("fsdp"),
        P("rep", "fsdp"),
        P("rep"),
    )
    out_specs = P("rep", "fsdp")
    return jax.shard_map(local, mesh=mesh, in_specs=in_specs, out_specs=out_specs, check_vma=False)
```

```python
import jax
import jax.numpy as jnp
from jax import lax
from jax.experimental import pallas as pl
from jax.experimental.pallas import tpu as pltpu
from jax.sharding import PartitionSpec as P

D = 8192
EPS = 1e-05
NX, NY, NC = 2, 8, 2
NZ, NH = 8, 4
SHARD = 16
PIECE = 64
HALF = 256
VMEM = pl.BlockSpec(memory_space=pltpu.VMEM)
SMEM = pl.BlockSpec(memory_space=pltpu.SMEM)
ANY = pl.BlockSpec(memory_space=pl.ANY)
PARAMS = pltpu.CompilerParams(vmem_limit_bytes=16 * 1024 * 1024)


def fsdp_of(x, y, c):
    return (x % NX * NY + y % NY) * NC + c % NC


def fsdp_perm(step):
    return [
        (fsdp_of(x, y, c), fsdp_of(*step(x, y, c)))
        for x in range(NX)
        for y in range(NY)
        for c in range(NC)
    ]


def rep_of(z, h):
    return z % NZ * NH + h % NH


def rep_perm(step):
    return [(rep_of(z, h), rep_of(*step(z, h))) for z in range(NZ) for h in range(NH)]


def even_partner(i):
    return i ^ 1


def odd_partner(i):
    return ((i + 1) ^ 1) - 1


def side_perm():
    moves = []
    for z in range(NZ):
        for h in range(NH):
            for f in range(NX * NY * NC):
                there = odd_partner(h) if f % NC else even_partner(h)
                width = NX * NY * NC
                moves.append((rep_of(z, h) * width + f, rep_of(z, there) * width + f))
    return moves


def chip_of(q, j):
    x = j // 2
    return x, (q + 2 * x) % 4 + 4 * (j % 2)


TEAMS = [[fsdp_of(*chip_of(q, j), c) for j in range(4)] for q in range(4) for c in range(NC)]
CLASSES = [
    [rep_of(z, h) for z in range(NZ) for h in range(NH) if (z + 2 * h) % 4 == q]
    for q in range(4)
]
BLOCKS = [fsdp_of(*chip_of(q, j), c) for c in range(NC) for q in range(4) for j in range(4)]


def piece_colors(me):
    x, y = me // (NY * NC), (me // NC) % NY
    own = (y + 2 * x) % 4
    to_even = 1 + 2 * (y % 2)
    return [own, (own + to_even) % 4, (own + 4 - to_even) % 4, (own + 2) % 4]


def piece_rows(first, color):
    return pl.ds(pl.multiple_of(first + color * PIECE, PIECE), PIECE)


def prep_kernel(len_ref, after_ref, res_ref, cot_ref, gain_ref, res_out, weighted_ref):
    gain = gain_ref[...].astype(jnp.float32)
    for i, block in enumerate(BLOCKS):
        token = block * SHARD + lax.broadcasted_iota(jnp.int32, (SHARD, 1), 0)
        live = (token < len_ref[0]).astype(jnp.float32)
        there = pl.ds(i * SHARD, SHARD)
        here = pl.ds(block * SHARD, SHARD)
        weighted_ref[there, :] = cot_ref[here, :].astype(jnp.float32) * gain * live
        res_out[there, :] = res_ref[here, :].astype(jnp.float32)


def product(pieces, w_ref):
    a = jnp.concatenate([piece[...] for piece in pieces], axis=0)
    return jnp.dot(a, w_ref[...], preferred_element_type=jnp.float32)


def near_kernel(p0, p1, p2, p3, w_ref, s_ref):
    s_ref[...] = product((p0, p1, p2, p3), w_ref)


def far_kernel(
    me_ref, p0, p1, p2, p3, w_ref, t_ref, near_s_ref, near_m_ref, res_ref, weighted_ref,
    stream_ref, moved_ref, stats_ref,
):
    me = me_ref[0]
    core = me % NC
    pieces = (p0, p1, p2, p3)
    s, m = product(pieces, w_ref), product(pieces, t_ref)
    for i, color in enumerate(piece_colors(me)):
        here = slice(i * PIECE, (i + 1) * PIECE)
        near = piece_rows(core * HALF, color)
        far = piece_rows((1 - core) * HALF, color)
        stream_ref[near, :] = near_s_ref[here, :]
        moved_ref[near, :] = near_m_ref[here, :]
        stream_ref[far, :] = s[here]
        moved_ref[far, :] = m[here]
    stream = stream_ref[...] + res_ref[...]
    stream_ref[...] = stream
    moved = moved_ref[...]
    weighted = weighted_ref[...]
    sums = [
        jnp.sum(stream * stream, axis=1, keepdims=True),
        jnp.sum(weighted * stream, axis=1, keepdims=True),
        jnp.sum(weighted * moved, axis=1, keepdims=True),
        jnp.sum(stream * moved, axis=1, keepdims=True),
    ]
    lane = lax.broadcasted_iota(jnp.int32, (2 * HALF, 128), 1)
    table = jnp.zeros((2 * HALF, 128), jnp.float32)
    for i, value in enumerate(sums):
        table = jnp.where(lane == i, value, table)
    turned = table.T
    packed = jnp.concatenate([turned[:4, :HALF], turned[:4, HALF:]], axis=0)
    for i in range(stats_ref.shape[0]):
        stats_ref[i] = packed


def second_kernel(
    ids_ref, stats_ref, stream_ref, moved_ref, weighted_ref,
    n0, n1, n2, n3, f0, f1, f2, f3,
    own_ref, side_ref, even_ref, odd_ref, curv_ref, a_ref, sems,
):
    copies = [
        pltpu.make_async_copy(piece, a_ref.at[pl.ds(i * PIECE, PIECE)], sems.at[i])
        for i, piece in enumerate((n0, n1, n2, n3, f0, f1, f2, f3))
    ]
    for copy in copies:
        copy.start()
    total = jnp.sum(stats_ref[...], axis=0)
    coefs = []
    for h in range(2):
        sum_sq, along_c, tangent_c, cross = (
            total[4 * h + i : 4 * h + i + 1] for i in range(4)
        )
        inv = lax.rsqrt(sum_sq / D + EPS)
        inv3 = inv * inv * inv
        inv5 = inv3 * inv * inv
        share = cross / D
        coefs.append(-inv3 * share)
        coefs.append((3.0 * inv5 * share * along_c - inv3 * tangent_c) / D)
        coefs.append(-inv3 * along_c / D)
    coefs.append(jnp.zeros((128 - len(coefs), HALF), jnp.float32))
    turned = jnp.concatenate(coefs, axis=0).T
    for h in range(2):
        rows = pl.ds(h * HALF, HALF)
        curv_ref[rows, :] = (
            turned[:, 3 * h : 3 * h + 1] * weighted_ref[rows, :]
            + turned[:, 3 * h + 1 : 3 * h + 2] * stream_ref[rows, :]
            + turned[:, 3 * h + 2 : 3 * h + 3] * moved_ref[rows, :]
        )
    me = ids_ref[0]
    core = me % NC
    colors = piece_colors(me)
    curv = jnp.concatenate(
        [curv_ref[piece_rows(core * HALF, q), :] for q in colors]
        + [curv_ref[piece_rows((1 - core) * HALF, q), :] for q in colors],
        axis=0,
    )
    curv_t = curv.T.astype(jnp.bfloat16)
    for copy in copies:
        copy.wait()
    color = ids_ref[1]
    to_even = 1 + 2 * (color % 2)
    for out_ref, step in (
        (side_ref, 2), (even_ref, to_even), (odd_ref, 4 - to_even), (own_ref, 0)
    ):
        q = (color + step) % 4
        for pair in range(4):
            z = 2 * pair + q % 2
            h = ((z - q + 8) % 4) // 2
            columns = []
            for k in range(2):
                at = pl.ds(pl.multiple_of((z * NH + h + 2 * k) * 128, 128), 128)
                columns.append(a_ref[:, at])
            out = jnp.dot(
                curv_t,
                jnp.concatenate(columns, axis=1),
                preferred_element_type=jnp.float32,
            ).astype(jnp.bfloat16)
            out_ref[2 * pair] = out[:, :128]
            out_ref[2 * pair + 1] = out[:, 128:]


def third_kernel(side_ref, own_ref, even_ref, odd_ref, out_ref):
    f32 = jnp.float32
    for i in range(own_ref.shape[0]):
        out_ref[i] = (
            own_ref[i].astype(f32)
            + even_ref[i].astype(f32)
            + odd_ref[i].astype(f32)
            + side_ref[i].astype(f32)
        ).astype(out_ref.dtype)


def last_kernel(parts_ref, out_ref):
    total = parts_ref[0].astype(jnp.float32)
    for i in range(1, parts_ref.shape[0]):
        total = total + parts_ref[i].astype(jnp.float32)
    out_ref[...] = total.T.astype(out_ref.dtype)


def local(attn_out, residual, out_weight, tangent, norm_gain, cotangent, seq_len):
    f32, bf16 = jnp.float32, jnp.bfloat16
    rows, columns = residual.shape
    features = attn_out.shape[1]
    me = lax.axis_index("fsdp")
    rep = lax.axis_index("rep")
    color = (rep // NH + 2 * (rep % NH)) % 4
    ids = jnp.stack([me, color]).astype(jnp.int32)
    gain = norm_gain[None, :]

    def in_group(x, step):
        return lax.ppermute(x, "fsdp", fsdp_perm(step))

    def of_groups(x, step):
        return lax.ppermute(x, "rep", rep_perm(step))

    def shape(*dims, dtype=f32):
        return jax.ShapeDtypeStruct(dims, dtype)

    own = lax.all_to_all(
        jnp.broadcast_to(attn_out[None], (4, SHARD, features)),
        "fsdp", 0, 0, axis_index_groups=TEAMS,
    ).reshape(PIECE, features)
    near = [
        own,
        in_group(own, lambda x, y, c: (x, even_partner(y), c)),
        in_group(own, lambda x, y, c: (x, odd_partner(y), c)),
        in_group(own, lambda x, y, c: (x + 1, y, c)),
    ]
    res, weighted = pl.pallas_call(
        prep_kernel,
        out_shape=(shape(rows, columns), shape(rows, columns)),
        in_specs=[SMEM, ANY, VMEM, VMEM, VMEM],
        out_specs=(VMEM,) * 2,
        compiler_params=PARAMS,
        name="prep",
    )(seq_len, own, residual, cotangent, gain)
    ready, res = lax.optimization_barrier((own, res))

    far = [in_group(piece, lambda x, y, c: (x, y, c + 1)) for piece in [ready] + near[1:]]

    near_s, near_m = (
        pl.pallas_call(
            near_kernel,
            out_shape=shape(HALF, columns),
            in_specs=[VMEM] * 5,
            out_specs=VMEM,
            compiler_params=PARAMS,
            name=name,
        )(*near, w)
        for name, w in (("near_s", out_weight), ("near_m", tangent))
    )

    stream, moved, stats = pl.pallas_call(
        far_kernel,
        out_shape=(shape(rows, columns), shape(rows, columns), shape(32, 8, HALF)),
        in_specs=[SMEM] + [VMEM] * 10,
        out_specs=(VMEM,) * 3,
        compiler_params=PARAMS,
        name="far",
    )(ids, *far, out_weight, tangent, near_s, near_m, res, weighted)

    stats = lax.all_to_all(stats, "fsdp", 0, 0)

    whole = shape(8, columns, 128, dtype=bf16)
    mine, side, even, odd = pl.pallas_call(
        second_kernel,
        out_shape=(whole,) * 4,
        in_specs=[SMEM] + [VMEM] * 4 + [ANY] * 8,
        out_specs=(VMEM,) * 4,
        scratch_shapes=[
            pltpu.VMEM((rows, columns), f32),
            pltpu.VMEM((rows, features), bf16),
            pltpu.SemaphoreType.DMA((8,)),
        ],
        compiler_params=PARAMS,
        name="second",
    )(ids, stats, stream, moved, weighted, *near, *far)

    side = lax.ppermute(side, ("rep", "fsdp"), side_perm())
    even = of_groups(even, lambda z, h: (even_partner(z), h))
    odd = of_groups(odd, lambda z, h: (odd_partner(z), h))
    four = pl.pallas_call(
        third_kernel,
        out_shape=whole,
        in_specs=[VMEM] * 4,
        out_specs=VMEM,
        compiler_params=PARAMS,
        name="third",
    )(side, mine, even, odd)
    parts = lax.all_to_all(four, "rep", 0, 0, axis_index_groups=CLASSES)
    return pl.pallas_call(
        last_kernel,
        out_shape=shape(128, columns, dtype=bf16),
        in_specs=[VMEM],
        out_specs=VMEM,
        compiler_params=PARAMS,
        name="last",
    )(parts)


def solution(mesh):
    in_specs = (
        P(("rep", "fsdp"), None),
        P("rep", "fsdp"),
        P(None, "fsdp"),
        P(None, "fsdp"),
        P("fsdp"),
        P("rep", "fsdp"),
        P("rep"),
    )
    out_specs = P("rep", "fsdp")
    return jax.shard_map(local, mesh=mesh, in_specs=in_specs, out_specs=out_specs, check_vma=False)
```

```python
import jax
import jax.numpy as jnp
from jax import lax
from jax.experimental import pallas as pl
from jax.experimental.pallas import tpu as pltpu
from jax.sharding import PartitionSpec as P

D = 8192
EPS = 1e-05
NX, NY, NC = 2, 8, 2
NZ, NH = 8, 4
SHARD = 16
PIECE = 64
HALF = 256
VMEM = pl.BlockSpec(memory_space=pltpu.VMEM)
SMEM = pl.BlockSpec(memory_space=pltpu.SMEM)
ANY = pl.BlockSpec(memory_space=pl.ANY)
PARAMS = pltpu.CompilerParams(vmem_limit_bytes=16 * 1024 * 1024)


def fsdp_of(x, y, c):
    return (x % NX * NY + y % NY) * NC + c % NC


def fsdp_perm(step):
    return [
        (fsdp_of(x, y, c), fsdp_of(*step(x, y, c)))
        for x in range(NX)
        for y in range(NY)
        for c in range(NC)
    ]


def rep_of(z, h):
    return z % NZ * NH + h % NH


def rep_perm(step):
    return [(rep_of(z, h), rep_of(*step(z, h))) for z in range(NZ) for h in range(NH)]


def even_partner(i):
    return i ^ 1


def odd_partner(i):
    return ((i + 1) ^ 1) - 1


def side_perm():
    moves = []
    for z in range(NZ):
        for h in range(NH):
            for f in range(NX * NY * NC):
                there = odd_partner(h) if f % NC else even_partner(h)
                width = NX * NY * NC
                moves.append((rep_of(z, h) * width + f, rep_of(z, there) * width + f))
    return moves


def chip_of(q, j):
    x = j // 2
    return x, (q + 2 * x) % 4 + 4 * (j % 2)


TEAMS = [[fsdp_of(*chip_of(q, j), c) for j in range(4)] for q in range(4) for c in range(NC)]
CLASSES = [
    [rep_of(z, h) for z in range(NZ) for h in range(NH) if (z + 2 * h) % 4 == q]
    for q in range(4)
]
BLOCKS = [fsdp_of(*chip_of(q, j), c) for c in range(NC) for q in range(4) for j in range(4)]


def piece_colors(me):
    x, y = me // (NY * NC), (me // NC) % NY
    own = (y + 2 * x) % 4
    to_even = 1 + 2 * (y % 2)
    return [own, (own + 2) % 4, (own + 4 - to_even) % 4, (own + to_even) % 4]


def piece_rows(first, color):
    return pl.ds(pl.multiple_of(first + color * PIECE, PIECE), PIECE)


def prep_kernel(len_ref, after_ref, res_ref, cot_ref, gain_ref, res_out, weighted_ref):
    gain = gain_ref[...].astype(jnp.float32)
    for i, block in enumerate(BLOCKS):
        token = block * SHARD + lax.broadcasted_iota(jnp.int32, (SHARD, 1), 0)
        live = (token < len_ref[0]).astype(jnp.float32)
        there = pl.ds(i * SHARD, SHARD)
        here = pl.ds(block * SHARD, SHARD)
        weighted_ref[there, :] = cot_ref[here, :].astype(jnp.float32) * gain * live
        res_out[there, :] = res_ref[here, :].astype(jnp.float32)


def product(pieces, w_ref):
    a = jnp.concatenate([piece[...] for piece in pieces], axis=0)
    return jnp.dot(a, w_ref[...], preferred_element_type=jnp.float32)


def near_kernel(p0, p1, p2, p3, w_ref, s_ref):
    s_ref[...] = product((p0, p1, p2, p3), w_ref)


def far_kernel(
    me_ref, p0, p1, p2, p3, w_ref, t_ref, near_s_ref, near_m_ref, res_ref, weighted_ref,
    stream_ref, moved_ref, stats_ref,
):
    me = me_ref[0]
    core = me % NC
    pieces = (p0, p1, p2, p3)
    s, m = product(pieces, w_ref), product(pieces, t_ref)
    for i, color in enumerate(piece_colors(me)):
        here = slice(i * PIECE, (i + 1) * PIECE)
        near = piece_rows(core * HALF, color)
        far = piece_rows((1 - core) * HALF, color)
        stream_ref[near, :] = near_s_ref[here, :]
        moved_ref[near, :] = near_m_ref[here, :]
        stream_ref[far, :] = s[here]
        moved_ref[far, :] = m[here]
    stream = stream_ref[...] + res_ref[...]
    stream_ref[...] = stream
    moved = moved_ref[...]
    weighted = weighted_ref[...]
    sums = [
        jnp.sum(stream * stream, axis=1, keepdims=True),
        jnp.sum(weighted * stream, axis=1, keepdims=True),
        jnp.sum(weighted * moved, axis=1, keepdims=True),
        jnp.sum(stream * moved, axis=1, keepdims=True),
    ]
    lane = lax.broadcasted_iota(jnp.int32, (2 * HALF, 128), 1)
    table = jnp.zeros((2 * HALF, 128), jnp.float32)
    for i, value in enumerate(sums):
        table = jnp.where(lane == i, value, table)
    turned = table.T
    packed = jnp.concatenate([turned[:4, :HALF], turned[:4, HALF:]], axis=0)
    for i in range(stats_ref.shape[0]):
        stats_ref[i] = packed


def second_kernel(
    ids_ref, stats_ref, stream_ref, moved_ref, weighted_ref,
    n0, n1, n2, n3, f0, f1, f2, f3,
    own_ref, side_ref, even_ref, odd_ref, curv_ref, a_ref, sems,
):
    copies = [
        pltpu.make_async_copy(piece, a_ref.at[pl.ds(i * PIECE, PIECE)], sems.at[i])
        for i, piece in enumerate((n0, n1, n2, n3, f0, f1, f2, f3))
    ]
    for copy in copies:
        copy.start()
    total = jnp.sum(stats_ref[...], axis=0)
    coefs = []
    for h in range(2):
        sum_sq, along_c, tangent_c, cross = (
            total[4 * h + i : 4 * h + i + 1] for i in range(4)
        )
        inv = lax.rsqrt(sum_sq / D + EPS)
        inv3 = inv * inv * inv
        inv5 = inv3 * inv * inv
        share = cross / D
        coefs.append(-inv3 * share)
        coefs.append((3.0 * inv5 * share * along_c - inv3 * tangent_c) / D)
        coefs.append(-inv3 * along_c / D)
    coefs.append(jnp.zeros((128 - len(coefs), HALF), jnp.float32))
    turned = jnp.concatenate(coefs, axis=0).T
    for h in range(2):
        rows = pl.ds(h * HALF, HALF)
        curv_ref[rows, :] = (
            turned[:, 3 * h : 3 * h + 1] * weighted_ref[rows, :]
            + turned[:, 3 * h + 1 : 3 * h + 2] * stream_ref[rows, :]
            + turned[:, 3 * h + 2 : 3 * h + 3] * moved_ref[rows, :]
        )
    me = ids_ref[0]
    core = me % NC
    colors = piece_colors(me)
    curv = jnp.concatenate(
        [curv_ref[piece_rows(core * HALF, q), :] for q in colors]
        + [curv_ref[piece_rows((1 - core) * HALF, q), :] for q in colors],
        axis=0,
    )
    curv_t = curv.T.astype(jnp.bfloat16)
    for copy in copies:
        copy.wait()
    color = ids_ref[1]
    to_even = 1 + 2 * (color % 2)
    for out_ref, step in (
        (side_ref, 2), (even_ref, to_even), (odd_ref, 4 - to_even), (own_ref, 0)
    ):
        q = (color + step) % 4
        for pair in range(4):
            z = 2 * pair + q % 2
            h = ((z - q + 8) % 4) // 2
            columns = []
            for k in range(2):
                at = pl.ds(pl.multiple_of((z * NH + h + 2 * k) * 128, 128), 128)
                columns.append(a_ref[:, at])
            out = jnp.dot(
                curv_t,
                jnp.concatenate(columns, axis=1),
                preferred_element_type=jnp.float32,
            ).astype(jnp.bfloat16)
            out_ref[2 * pair] = out[:, :128]
            out_ref[2 * pair + 1] = out[:, 128:]


def third_kernel(own_ref, even_ref, odd_ref, side_ref, out_ref):
    f32 = jnp.float32
    for i in range(own_ref.shape[0]):
        out_ref[i] = (
            own_ref[i].astype(f32)
            + even_ref[i].astype(f32)
            + odd_ref[i].astype(f32)
            + side_ref[i].astype(f32)
        ).astype(out_ref.dtype)


def last_kernel(parts_ref, out_ref):
    total = parts_ref[0].astype(jnp.float32)
    for i in range(1, parts_ref.shape[0]):
        total = total + parts_ref[i].astype(jnp.float32)
    out_ref[...] = total.T.astype(out_ref.dtype)


def local(attn_out, residual, out_weight, tangent, norm_gain, cotangent, seq_len):
    f32, bf16 = jnp.float32, jnp.bfloat16
    rows, columns = residual.shape
    features = attn_out.shape[1]
    me = lax.axis_index("fsdp")
    rep = lax.axis_index("rep")
    color = (rep // NH + 2 * (rep % NH)) % 4
    ids = jnp.stack([me, color]).astype(jnp.int32)
    gain = norm_gain[None, :]

    def in_group(x, step):
        return lax.ppermute(x, "fsdp", fsdp_perm(step))

    def of_groups(x, step):
        return lax.ppermute(x, "rep", rep_perm(step))

    def shape(*dims, dtype=f32):
        return jax.ShapeDtypeStruct(dims, dtype)

    own = lax.all_to_all(
        jnp.broadcast_to(attn_out[None], (4, SHARD, features)),
        "fsdp", 0, 0, axis_index_groups=TEAMS,
    ).reshape(PIECE, features)
    near = [
        own,
        in_group(own, lambda x, y, c: (x + 1, y, c)),
        in_group(own, lambda x, y, c: (x, odd_partner(y), c)),
        in_group(own, lambda x, y, c: (x, even_partner(y), c)),
    ]
    res, weighted = pl.pallas_call(
        prep_kernel,
        out_shape=(shape(rows, columns), shape(rows, columns)),
        in_specs=[SMEM, ANY, VMEM, VMEM, VMEM],
        out_specs=(VMEM,) * 2,
        compiler_params=PARAMS,
        name="prep",
    )(seq_len, own, residual, cotangent, gain)
    ready, res = lax.optimization_barrier((own, res))

    far = [in_group(piece, lambda x, y, c: (x, y, c + 1)) for piece in [ready] + near[1:]]

    near_s, near_m = (
        pl.pallas_call(
            near_kernel,
            out_shape=shape(HALF, columns),
            in_specs=[VMEM] * 5,
            out_specs=VMEM,
            compiler_params=PARAMS,
            name=name,
        )(*near, w)
        for name, w in (("near_s", out_weight), ("near_m", tangent))
    )

    stream, moved, stats = pl.pallas_call(
        far_kernel,
        out_shape=(shape(rows, columns), shape(rows, columns), shape(32, 8, HALF)),
        in_specs=[SMEM] + [VMEM] * 10,
        out_specs=(VMEM,) * 3,
        compiler_params=PARAMS,
        name="far",
    )(ids, *far, out_weight, tangent, near_s, near_m, res, weighted)

    stats = lax.all_to_all(stats, "fsdp", 0, 0)

    whole = shape(8, columns, 128, dtype=bf16)
    mine, side, even, odd = pl.pallas_call(
        second_kernel,
        out_shape=(whole,) * 4,
        in_specs=[SMEM] + [VMEM] * 4 + [ANY] * 8,
        out_specs=(VMEM,) * 4,
        scratch_shapes=[
            pltpu.VMEM((rows, columns), f32),
            pltpu.VMEM((rows, features), bf16),
            pltpu.SemaphoreType.DMA((8,)),
        ],
        compiler_params=PARAMS,
        name="second",
    )(ids, stats, stream, moved, weighted, *near, *far)

    side = lax.ppermute(side, ("rep", "fsdp"), side_perm())
    even = of_groups(even, lambda z, h: (even_partner(z), h))
    odd = of_groups(odd, lambda z, h: (odd_partner(z), h))
    four = pl.pallas_call(
        third_kernel,
        out_shape=whole,
        in_specs=[VMEM] * 4,
        out_specs=VMEM,
        compiler_params=PARAMS,
        name="third",
    )(mine, even, odd, side)
    parts = lax.all_to_all(four, "rep", 0, 0, axis_index_groups=CLASSES)
    return pl.pallas_call(
        last_kernel,
        out_shape=shape(128, columns, dtype=bf16),
        in_specs=[VMEM],
        out_specs=VMEM,
        compiler_params=PARAMS,
        name="last",
    )(parts)


def solution(mesh):
    in_specs = (
        P(("rep", "fsdp"), None),
        P("rep", "fsdp"),
        P(None, "fsdp"),
        P(None, "fsdp"),
        P("fsdp"),
        P("rep", "fsdp"),
        P("rep"),
    )
    out_specs = P("rep", "fsdp")
    return jax.shard_map(local, mesh=mesh, in_specs=in_specs, out_specs=out_specs, check_vma=False)
```

```python
import jax
import jax.numpy as jnp
from jax import lax
from jax.experimental import pallas as pl
from jax.experimental.pallas import tpu as pltpu
from jax.sharding import PartitionSpec as P

D = 8192
EPS = 1e-05
NX, NY, NC = 2, 8, 2
NZ, NH = 8, 4
SHARD = 16
PIECE = 64
HALF = 256
VMEM = pl.BlockSpec(memory_space=pltpu.VMEM)
SMEM = pl.BlockSpec(memory_space=pltpu.SMEM)
ANY = pl.BlockSpec(memory_space=pl.ANY)
PARAMS = pltpu.CompilerParams(vmem_limit_bytes=16 * 1024 * 1024)


def fsdp_of(x, y, c):
    return (x % NX * NY + y % NY) * NC + c % NC


def fsdp_perm(step):
    return [
        (fsdp_of(x, y, c), fsdp_of(*step(x, y, c)))
        for x in range(NX)
        for y in range(NY)
        for c in range(NC)
    ]


def rep_of(z, h):
    return z % NZ * NH + h % NH


def rep_perm(step):
    return [(rep_of(z, h), rep_of(*step(z, h))) for z in range(NZ) for h in range(NH)]


def even_partner(i):
    return i ^ 1


def odd_partner(i):
    return ((i + 1) ^ 1) - 1


def side_perm():
    moves = []
    for z in range(NZ):
        for h in range(NH):
            for f in range(NX * NY * NC):
                there = odd_partner(h) if f % NC else even_partner(h)
                width = NX * NY * NC
                moves.append((rep_of(z, h) * width + f, rep_of(z, there) * width + f))
    return moves


def chip_of(q, j):
    x = j // 2
    return x, (q + 2 * x) % 4 + 4 * (j % 2)


TEAMS = [[fsdp_of(*chip_of(q, j), c) for j in range(4)] for q in range(4) for c in range(NC)]
CLASSES = [
    [rep_of(z, h) for z in range(NZ) for h in range(NH) if (z + 2 * h) % 4 == q]
    for q in range(4)
]
BLOCKS = [fsdp_of(*chip_of(q, j), c) for c in range(NC) for q in range(4) for j in range(4)]


def piece_colors(me):
    x, y = me // (NY * NC), (me // NC) % NY
    own = (y + 2 * x) % 4
    to_even = 1 + 2 * (y % 2)
    return [own, (own + 2) % 4, (own + 4 - to_even) % 4, (own + to_even) % 4]


def piece_rows(first, color):
    return pl.ds(pl.multiple_of(first + color * PIECE, PIECE), PIECE)


def product(pieces, w_ref):
    a = jnp.concatenate([piece[...] for piece in pieces], axis=0)
    return jnp.dot(a, w_ref[...], preferred_element_type=jnp.float32)


def near_kernel(p0, p1, p2, p3, w_ref, s_ref):
    s_ref[...] = product((p0, p1, p2, p3), w_ref)


def far_kernel(
    me_ref, len_ref, p0, p1, p2, p3, w_ref, t_ref, near_s_ref, near_m_ref,
    res_ref, cot_ref, gain_ref,
    stream_ref, moved_ref, weighted_ref, stats_ref,
):
    me = me_ref[0]
    core = me % NC
    pieces = (p0, p1, p2, p3)
    s, m = product(pieces, w_ref), product(pieces, t_ref)
    for i, color in enumerate(piece_colors(me)):
        here = slice(i * PIECE, (i + 1) * PIECE)
        near = piece_rows(core * HALF, color)
        far = piece_rows((1 - core) * HALF, color)
        stream_ref[near, :] = near_s_ref[here, :]
        moved_ref[near, :] = near_m_ref[here, :]
        stream_ref[far, :] = s[here]
        moved_ref[far, :] = m[here]
    gain = gain_ref[...].astype(jnp.float32)
    for i, block in enumerate(BLOCKS):
        token = block * SHARD + lax.broadcasted_iota(jnp.int32, (SHARD, 1), 0)
        live = (token < len_ref[0]).astype(jnp.float32)
        there = pl.ds(i * SHARD, SHARD)
        here = pl.ds(block * SHARD, SHARD)
        weighted_ref[there, :] = cot_ref[here, :].astype(jnp.float32) * gain * live
        stream_ref[there, :] += res_ref[here, :].astype(jnp.float32)
    stream = stream_ref[...]
    moved = moved_ref[...]
    weighted = weighted_ref[...]
    sums = [
        jnp.sum(stream * stream, axis=1, keepdims=True),
        jnp.sum(weighted * stream, axis=1, keepdims=True),
        jnp.sum(weighted * moved, axis=1, keepdims=True),
        jnp.sum(stream * moved, axis=1, keepdims=True),
    ]
    lane = lax.broadcasted_iota(jnp.int32, (2 * HALF, 128), 1)
    table = jnp.zeros((2 * HALF, 128), jnp.float32)
    for i, value in enumerate(sums):
        table = jnp.where(lane == i, value, table)
    turned = table.T
    packed = jnp.concatenate([turned[:4, :HALF], turned[:4, HALF:]], axis=0)
    for i in range(stats_ref.shape[0]):
        stats_ref[i] = packed


def second_kernel(
    ids_ref, stats_ref, stream_ref, moved_ref, weighted_ref,
    n0, n1, n2, n3, f0, f1, f2, f3,
    own_ref, side_ref, even_ref, odd_ref, curv_ref, a_ref, sems,
):
    copies = [
        pltpu.make_async_copy(piece, a_ref.at[pl.ds(i * PIECE, PIECE)], sems.at[i])
        for i, piece in enumerate((n0, n1, n2, n3, f0, f1, f2, f3))
    ]
    for copy in copies:
        copy.start()
    total = jnp.sum(stats_ref[...], axis=0)
    coefs = []
    for h in range(2):
        sum_sq, along_c, tangent_c, cross = (
            total[4 * h + i : 4 * h + i + 1] for i in range(4)
        )
        inv = lax.rsqrt(sum_sq / D + EPS)
        inv3 = inv * inv * inv
        inv5 = inv3 * inv * inv
        share = cross / D
        coefs.append(-inv3 * share)
        coefs.append((3.0 * inv5 * share * along_c - inv3 * tangent_c) / D)
        coefs.append(-inv3 * along_c / D)
    coefs.append(jnp.zeros((128 - len(coefs), HALF), jnp.float32))
    turned = jnp.concatenate(coefs, axis=0).T
    for h in range(2):
        rows = pl.ds(h * HALF, HALF)
        curv_ref[rows, :] = (
            turned[:, 3 * h : 3 * h + 1] * weighted_ref[rows, :]
            + turned[:, 3 * h + 1 : 3 * h + 2] * stream_ref[rows, :]
            + turned[:, 3 * h + 2 : 3 * h + 3] * moved_ref[rows, :]
        )
    me = ids_ref[0]
    core = me % NC
    colors = piece_colors(me)
    curv = jnp.concatenate(
        [curv_ref[piece_rows(core * HALF, q), :] for q in colors]
        + [curv_ref[piece_rows((1 - core) * HALF, q), :] for q in colors],
        axis=0,
    )
    curv_t = curv.T.astype(jnp.bfloat16)
    for copy in copies:
        copy.wait()
    color = ids_ref[1]
    to_even = 1 + 2 * (color % 2)
    for out_ref, step in (
        (side_ref, 2), (even_ref, to_even), (odd_ref, 4 - to_even), (own_ref, 0)
    ):
        q = (color + step) % 4
        for pair in range(4):
            z = 2 * pair + q % 2
            h = ((z - q + 8) % 4) // 2
            columns = []
            for k in range(2):
                at = pl.ds(pl.multiple_of((z * NH + h + 2 * k) * 128, 128), 128)
                columns.append(a_ref[:, at])
            out = jnp.dot(
                curv_t,
                jnp.concatenate(columns, axis=1),
                preferred_element_type=jnp.float32,
            ).astype(jnp.bfloat16)
            out_ref[2 * pair] = out[:, :128]
            out_ref[2 * pair + 1] = out[:, 128:]


def third_kernel(own_ref, even_ref, odd_ref, side_ref, out_ref):
    f32 = jnp.float32
    for i in range(own_ref.shape[0]):
        out_ref[i] = (
            own_ref[i].astype(f32)
            + even_ref[i].astype(f32)
            + odd_ref[i].astype(f32)
            + side_ref[i].astype(f32)
        ).astype(out_ref.dtype)


def last_kernel(parts_ref, out_ref):
    total = parts_ref[0].astype(jnp.float32)
    for i in range(1, parts_ref.shape[0]):
        total = total + parts_ref[i].astype(jnp.float32)
    out_ref[...] = total.T.astype(out_ref.dtype)


def local(attn_out, residual, out_weight, tangent, norm_gain, cotangent, seq_len):
    f32, bf16 = jnp.float32, jnp.bfloat16
    rows, columns = residual.shape
    features = attn_out.shape[1]
    me = lax.axis_index("fsdp")
    rep = lax.axis_index("rep")
    color = (rep // NH + 2 * (rep % NH)) % 4
    ids = jnp.stack([me, color]).astype(jnp.int32)
    gain = norm_gain[None, :]

    def in_group(x, step):
        return lax.ppermute(x, "fsdp", fsdp_perm(step))

    def of_groups(x, step):
        return lax.ppermute(x, "rep", rep_perm(step))

    def shape(*dims, dtype=f32):
        return jax.ShapeDtypeStruct(dims, dtype)

    own = lax.all_to_all(
        jnp.broadcast_to(attn_out[None], (4, SHARD, features)),
        "fsdp", 0, 0, axis_index_groups=TEAMS,
    ).reshape(PIECE, features)
    near = [
        own,
        in_group(own, lambda x, y, c: (x + 1, y, c)),
        in_group(own, lambda x, y, c: (x, odd_partner(y), c)),
        in_group(own, lambda x, y, c: (x, even_partner(y), c)),
    ]
    near[3], gain = lax.optimization_barrier((near[3], gain))
    far = [in_group(piece, lambda x, y, c: (x, y, c + 1)) for piece in near]

    near_s, near_m = (
        pl.pallas_call(
            near_kernel,
            out_shape=shape(HALF, columns),
            in_specs=[VMEM] * 5,
            out_specs=VMEM,
            compiler_params=PARAMS,
            name=name,
        )(*near, w)
        for name, w in (("near_s", out_weight), ("near_m", tangent))
    )

    whole = shape(rows, columns)
    stream, moved, weighted, stats = pl.pallas_call(
        far_kernel,
        out_shape=(whole, whole, whole, shape(32, 8, HALF)),
        in_specs=[SMEM, SMEM] + [VMEM] * 11,
        out_specs=(VMEM,) * 4,
        compiler_params=PARAMS,
        name="far",
    )(
        ids, seq_len, *far, out_weight, tangent, near_s, near_m,
        residual, cotangent, gain,
    )

    stats = lax.all_to_all(stats, "fsdp", 0, 0)

    whole = shape(8, columns, 128, dtype=bf16)
    mine, side, even, odd = pl.pallas_call(
        second_kernel,
        out_shape=(whole,) * 4,
        in_specs=[SMEM] + [VMEM] * 4 + [ANY] * 8,
        out_specs=(VMEM,) * 4,
        scratch_shapes=[
            pltpu.VMEM((rows, columns), f32),
            pltpu.VMEM((rows, features), bf16),
            pltpu.SemaphoreType.DMA((8,)),
        ],
        compiler_params=PARAMS,
        name="second",
    )(ids, stats, stream, moved, weighted, *near, *far)

    side = lax.ppermute(side, ("rep", "fsdp"), side_perm())
    even = of_groups(even, lambda z, h: (even_partner(z), h))
    odd = of_groups(odd, lambda z, h: (odd_partner(z), h))
    four = pl.pallas_call(
        third_kernel,
        out_shape=whole,
        in_specs=[VMEM] * 4,
        out_specs=VMEM,
        compiler_params=PARAMS,
        name="third",
    )(mine, even, odd, side)
    parts = lax.all_to_all(four, "rep", 0, 0, axis_index_groups=CLASSES)
    return pl.pallas_call(
        last_kernel,
        out_shape=shape(128, columns, dtype=bf16),
        in_specs=[VMEM],
        out_specs=VMEM,
        compiler_params=PARAMS,
        name="last",
    )(parts)


def solution(mesh):
    in_specs = (
        P(("rep", "fsdp"), None),
        P("rep", "fsdp"),
        P(None, "fsdp"),
        P(None, "fsdp"),
        P("fsdp"),
        P("rep", "fsdp"),
        P("rep"),
    )
    out_specs = P("rep", "fsdp")
    return jax.shard_map(local, mesh=mesh, in_specs=in_specs, out_specs=out_specs, check_vma=False)
```

```python
import jax
import jax.numpy as jnp
from jax import lax
from jax.experimental import pallas as pl
from jax.experimental.pallas import tpu as pltpu
from jax.sharding import PartitionSpec as P

D = 8192
EPS = 1e-05
NX, NY, NC = 2, 8, 2
NZ, NH = 8, 4
SHARD = 16
PIECE = 64
HALF = 256
VMEM = pl.BlockSpec(memory_space=pltpu.VMEM)
SMEM = pl.BlockSpec(memory_space=pltpu.SMEM)
ANY = pl.BlockSpec(memory_space=pl.ANY)
PARAMS = pltpu.CompilerParams(vmem_limit_bytes=16 * 1024 * 1024)


def fsdp_of(x, y, c):
    return (x % NX * NY + y % NY) * NC + c % NC


def fsdp_perm(step):
    return [
        (fsdp_of(x, y, c), fsdp_of(*step(x, y, c)))
        for x in range(NX)
        for y in range(NY)
        for c in range(NC)
    ]


def rep_of(z, h):
    return z % NZ * NH + h % NH


def rep_perm(step):
    return [(rep_of(z, h), rep_of(*step(z, h))) for z in range(NZ) for h in range(NH)]


def even_partner(i):
    return i ^ 1


def odd_partner(i):
    return ((i + 1) ^ 1) - 1


def side_perm():
    moves = []
    for z in range(NZ):
        for h in range(NH):
            for f in range(NX * NY * NC):
                there = odd_partner(h) if f % NC else even_partner(h)
                width = NX * NY * NC
                moves.append((rep_of(z, h) * width + f, rep_of(z, there) * width + f))
    return moves


def chip_of(q, j):
    x = j // 2
    return x, (q + 2 * x) % 4 + 4 * (j % 2)


TEAMS = [[fsdp_of(*chip_of(q, j), c) for j in range(4)] for q in range(4) for c in range(NC)]
CLASSES = [
    [rep_of(z, h) for z in range(NZ) for h in range(NH) if (z + 2 * h) % 4 == q]
    for q in range(4)
]
BLOCKS = [fsdp_of(*chip_of(q, j), c) for c in range(NC) for q in range(4) for j in range(4)]


def piece_colors(me):
    x, y = me // (NY * NC), (me // NC) % NY
    own = (y + 2 * x) % 4
    to_even = 1 + 2 * (y % 2)
    return [own, (own + to_even) % 4, (own + 4 - to_even) % 4, (own + 2) % 4]


def piece_rows(first, color):
    return pl.ds(pl.multiple_of(first + color * PIECE, PIECE), PIECE)


def product(pieces, w_ref):
    a = jnp.concatenate([piece[...] for piece in pieces], axis=0)
    return jnp.dot(a, w_ref[...], preferred_element_type=jnp.float32)


def near_kernel(p0, p1, p2, p3, w_ref, s_ref):
    s_ref[...] = product((p0, p1, p2, p3), w_ref)


def far_kernel(
    me_ref, len_ref, p0, p1, p2, p3, w_ref, t_ref, near_s_ref, near_m_ref,
    res_ref, cot_ref, gain_ref,
    stream_ref, moved_ref, weighted_ref, stats_ref,
):
    me = me_ref[0]
    core = me % NC
    pieces = (p0, p1, p2, p3)
    s, m = product(pieces, w_ref), product(pieces, t_ref)
    for i, color in enumerate(piece_colors(me)):
        here = slice(i * PIECE, (i + 1) * PIECE)
        near = piece_rows(core * HALF, color)
        far = piece_rows((1 - core) * HALF, color)
        stream_ref[near, :] = near_s_ref[here, :]
        moved_ref[near, :] = near_m_ref[here, :]
        stream_ref[far, :] = s[here]
        moved_ref[far, :] = m[here]
    gain = gain_ref[...].astype(jnp.float32)
    for i, block in enumerate(BLOCKS):
        token = block * SHARD + lax.broadcasted_iota(jnp.int32, (SHARD, 1), 0)
        live = (token < len_ref[0]).astype(jnp.float32)
        there = pl.ds(i * SHARD, SHARD)
        here = pl.ds(block * SHARD, SHARD)
        weighted_ref[there, :] = cot_ref[here, :].astype(jnp.float32) * gain * live
        stream_ref[there, :] += res_ref[here, :].astype(jnp.float32)
    stream = stream_ref[...]
    moved = moved_ref[...]
    weighted = weighted_ref[...]
    sums = [
        jnp.sum(stream * stream, axis=1, keepdims=True),
        jnp.sum(weighted * stream, axis=1, keepdims=True),
        jnp.sum(weighted * moved, axis=1, keepdims=True),
        jnp.sum(stream * moved, axis=1, keepdims=True),
    ]
    lane = lax.broadcasted_iota(jnp.int32, (2 * HALF, 128), 1)
    table = jnp.zeros((2 * HALF, 128), jnp.float32)
    for i, value in enumerate(sums):
        table = jnp.where(lane == i, value, table)
    turned = table.T
    packed = jnp.concatenate([turned[:4, :HALF], turned[:4, HALF:]], axis=0)
    for i in range(stats_ref.shape[0]):
        stats_ref[i] = packed


def second_kernel(
    ids_ref, stats_ref, stream_ref, moved_ref, weighted_ref,
    n0, n1, n2, n3, f0, f1, f2, f3,
    own_ref, side_ref, even_ref, odd_ref, curv_ref, a_ref, sems,
):
    copies = [
        pltpu.make_async_copy(piece, a_ref.at[pl.ds(i * PIECE, PIECE)], sems.at[i])
        for i, piece in enumerate((n0, n1, n2, n3, f0, f1, f2, f3))
    ]
    for copy in copies:
        copy.start()
    total = jnp.sum(stats_ref[...], axis=0)
    coefs = []
    for h in range(2):
        sum_sq, along_c, tangent_c, cross = (
            total[4 * h + i : 4 * h + i + 1] for i in range(4)
        )
        inv = lax.rsqrt(sum_sq / D + EPS)
        inv3 = inv * inv * inv
        inv5 = inv3 * inv * inv
        share = cross / D
        coefs.append(-inv3 * share)
        coefs.append((3.0 * inv5 * share * along_c - inv3 * tangent_c) / D)
        coefs.append(-inv3 * along_c / D)
    coefs.append(jnp.zeros((128 - len(coefs), HALF), jnp.float32))
    turned = jnp.concatenate(coefs, axis=0).T
    for h in range(2):
        rows = pl.ds(h * HALF, HALF)
        curv_ref[rows, :] = (
            turned[:, 3 * h : 3 * h + 1] * weighted_ref[rows, :]
            + turned[:, 3 * h + 1 : 3 * h + 2] * stream_ref[rows, :]
            + turned[:, 3 * h + 2 : 3 * h + 3] * moved_ref[rows, :]
        )
    me = ids_ref[0]
    core = me % NC
    colors = piece_colors(me)
    curv = jnp.concatenate(
        [curv_ref[piece_rows(core * HALF, q), :] for q in colors]
        + [curv_ref[piece_rows((1 - core) * HALF, q), :] for q in colors],
        axis=0,
    )
    curv_t = curv.T.astype(jnp.bfloat16)
    for copy in copies:
        copy.wait()
    color = ids_ref[1]
    to_even = 1 + 2 * (color % 2)
    for out_ref, step in (
        (side_ref, 2), (even_ref, to_even), (odd_ref, 4 - to_even), (own_ref, 0)
    ):
        q = (color + step) % 4
        for pair in range(4):
            z = 2 * pair + q % 2
            h = ((z - q + 8) % 4) // 2
            columns = []
            for k in range(2):
                at = pl.ds(pl.multiple_of((z * NH + h + 2 * k) * 128, 128), 128)
                columns.append(a_ref[:, at])
            out = jnp.dot(
                curv_t,
                jnp.concatenate(columns, axis=1),
                preferred_element_type=jnp.float32,
            ).astype(jnp.bfloat16)
            out_ref[2 * pair] = out[:, :128]
            out_ref[2 * pair + 1] = out[:, 128:]


def third_kernel(side_ref, own_ref, even_ref, odd_ref, out_ref):
    f32 = jnp.float32
    for i in range(own_ref.shape[0]):
        out_ref[i] = (
            own_ref[i].astype(f32)
            + even_ref[i].astype(f32)
            + odd_ref[i].astype(f32)
            + side_ref[i].astype(f32)
        ).astype(out_ref.dtype)


def last_kernel(parts_ref, out_ref):
    total = parts_ref[0].astype(jnp.float32)
    for i in range(1, parts_ref.shape[0]):
        total = total + parts_ref[i].astype(jnp.float32)
    out_ref[...] = total.T.astype(out_ref.dtype)


def local(attn_out, residual, out_weight, tangent, norm_gain, cotangent, seq_len):
    f32, bf16 = jnp.float32, jnp.bfloat16
    rows, columns = residual.shape
    features = attn_out.shape[1]
    me = lax.axis_index("fsdp")
    rep = lax.axis_index("rep")
    color = (rep // NH + 2 * (rep % NH)) % 4
    ids = jnp.stack([me, color]).astype(jnp.int32)
    gain = norm_gain[None, :]

    def in_group(x, step):
        return lax.ppermute(x, "fsdp", fsdp_perm(step))

    def of_groups(x, step):
        return lax.ppermute(x, "rep", rep_perm(step))

    def shape(*dims, dtype=f32):
        return jax.ShapeDtypeStruct(dims, dtype)

    own = lax.all_to_all(
        jnp.broadcast_to(attn_out[None], (4, SHARD, features)),
        "fsdp", 0, 0, axis_index_groups=TEAMS,
    ).reshape(PIECE, features)
    near = [
        own,
        in_group(own, lambda x, y, c: (x, even_partner(y), c)),
        in_group(own, lambda x, y, c: (x, odd_partner(y), c)),
        in_group(own, lambda x, y, c: (x + 1, y, c)),
    ]
    ready, gain, ids = lax.optimization_barrier((own, gain, ids))
    far = [in_group(piece, lambda x, y, c: (x, y, c + 1)) for piece in [ready] + near[1:]]

    near_s, near_m = (
        pl.pallas_call(
            near_kernel,
            out_shape=shape(HALF, columns),
            in_specs=[VMEM] * 5,
            out_specs=VMEM,
            compiler_params=PARAMS,
            name=name,
        )(*near, w)
        for name, w in (("near_s", out_weight), ("near_m", tangent))
    )

    whole = shape(rows, columns)
    stream, moved, weighted, stats = pl.pallas_call(
        far_kernel,
        out_shape=(whole, whole, whole, shape(32, 8, HALF)),
        in_specs=[SMEM, SMEM] + [VMEM] * 11,
        out_specs=(VMEM,) * 4,
        compiler_params=PARAMS,
        name="far",
    )(
        ids, seq_len, *far, out_weight, tangent, near_s, near_m,
        residual, cotangent, gain,
    )

    stats = lax.all_to_all(stats, "fsdp", 0, 0)

    whole = shape(8, columns, 128, dtype=bf16)
    mine, side, even, odd = pl.pallas_call(
        second_kernel,
        out_shape=(whole,) * 4,
        in_specs=[SMEM] + [VMEM] * 4 + [ANY] * 8,
        out_specs=(VMEM,) * 4,
        scratch_shapes=[
            pltpu.VMEM((rows, columns), f32),
            pltpu.VMEM((rows, features), bf16),
            pltpu.SemaphoreType.DMA((8,)),
        ],
        compiler_params=PARAMS,
        name="second",
    )(ids, stats, stream, moved, weighted, *near, *far)

    side = lax.ppermute(side, ("rep", "fsdp"), side_perm())
    even = of_groups(even, lambda z, h: (even_partner(z), h))
    odd = of_groups(odd, lambda z, h: (odd_partner(z), h))
    four = pl.pallas_call(
        third_kernel,
        out_shape=whole,
        in_specs=[VMEM] * 4,
        out_specs=VMEM,
        compiler_params=PARAMS,
        name="third",
    )(side, mine, even, odd)
    parts = lax.all_to_all(four, "rep", 0, 0, axis_index_groups=CLASSES)
    return pl.pallas_call(
        last_kernel,
        out_shape=shape(128, columns, dtype=bf16),
        in_specs=[VMEM],
        out_specs=VMEM,
        compiler_params=PARAMS,
        name="last",
    )(parts)


def solution(mesh):
    in_specs = (
        P(("rep", "fsdp"), None),
        P("rep", "fsdp"),
        P(None, "fsdp"),
        P(None, "fsdp"),
        P("fsdp"),
        P("rep", "fsdp"),
        P("rep"),
    )
    out_specs = P("rep", "fsdp")
    return jax.shard_map(local, mesh=mesh, in_specs=in_specs, out_specs=out_specs, check_vma=False)
```

```python
import jax
import jax.numpy as jnp
from jax import lax
from jax.experimental import pallas as pl
from jax.experimental.pallas import tpu as pltpu
from jax.sharding import PartitionSpec as P

D = 8192
EPS = 1e-05
NX, NY, NC = 2, 8, 2
NZ, NH = 8, 4
SHARD = 16
PIECE = 64
HALF = 256
VMEM = pl.BlockSpec(memory_space=pltpu.VMEM)
SMEM = pl.BlockSpec(memory_space=pltpu.SMEM)
ANY = pl.BlockSpec(memory_space=pl.ANY)
PARAMS = pltpu.CompilerParams(vmem_limit_bytes=16 * 1024 * 1024)


def fsdp_of(x, y, c):
    return (x % NX * NY + y % NY) * NC + c % NC


def fsdp_perm(step):
    return [
        (fsdp_of(x, y, c), fsdp_of(*step(x, y, c)))
        for x in range(NX)
        for y in range(NY)
        for c in range(NC)
    ]


def rep_of(z, h):
    return z % NZ * NH + h % NH


def rep_perm(step):
    return [(rep_of(z, h), rep_of(*step(z, h))) for z in range(NZ) for h in range(NH)]


def even_partner(i):
    return i ^ 1


def odd_partner(i):
    return ((i + 1) ^ 1) - 1


def side_perm():
    moves = []
    for z in range(NZ):
        for h in range(NH):
            for f in range(NX * NY * NC):
                there = odd_partner(h) if f % NC else even_partner(h)
                width = NX * NY * NC
                moves.append((rep_of(z, h) * width + f, rep_of(z, there) * width + f))
    return moves


def chip_of(q, j):
    x = j // 2
    return x, (q + 2 * x) % 4 + 4 * (j % 2)


TEAMS = [[fsdp_of(*chip_of(q, j), c) for j in range(4)] for q in range(4) for c in range(NC)]
CLASSES = [
    [rep_of(z, h) for z in range(NZ) for h in range(NH) if (z + 2 * h) % 4 == q]
    for q in range(4)
]
BLOCKS = [fsdp_of(*chip_of(q, j), c) for c in range(NC) for q in range(4) for j in range(4)]


def piece_colors(me):
    x, y = me // (NY * NC), (me // NC) % NY
    own = (y + 2 * x) % 4
    to_even = 1 + 2 * (y % 2)
    return [own, (own + to_even) % 4, (own + 4 - to_even) % 4, (own + 2) % 4]


def piece_rows(first, color):
    return pl.ds(pl.multiple_of(first + color * PIECE, PIECE), PIECE)


def product(pieces, w_ref):
    a = jnp.concatenate([piece[...] for piece in pieces], axis=0)
    return jnp.dot(a, w_ref[...], preferred_element_type=jnp.float32)


def near_kernel(p0, p1, p2, p3, w_ref, s_ref):
    s_ref[...] = product((p0, p1, p2, p3), w_ref)


def far_kernel(
    me_ref, len_ref, n0, n1, n2, n3, f0, f1, f2, f3, w_ref, t_ref, near_s_ref,
    res_ref, cot_ref, gain_ref,
    stream_ref, moved_ref, weighted_ref, stats_ref,
):
    me = me_ref[0]
    core = me % NC
    near, far = (n0, n1, n2, n3), (f0, f1, f2, f3)
    for first, target, value in (
        (core, stream_ref, near_s_ref[...]),
        (1 - core, stream_ref, product(far, w_ref)),
        (core, moved_ref, product(near, t_ref)),
        (1 - core, moved_ref, product(far, t_ref)),
    ):
        for i, color in enumerate(piece_colors(me)):
            target[piece_rows(first * HALF, color), :] = value[i * PIECE : (i + 1) * PIECE]
    gain = gain_ref[...].astype(jnp.float32)
    for i, block in enumerate(BLOCKS):
        token = block * SHARD + lax.broadcasted_iota(jnp.int32, (SHARD, 1), 0)
        live = (token < len_ref[0]).astype(jnp.float32)
        there = pl.ds(i * SHARD, SHARD)
        here = pl.ds(block * SHARD, SHARD)
        weighted_ref[there, :] = cot_ref[here, :].astype(jnp.float32) * gain * live
        stream_ref[there, :] += res_ref[here, :].astype(jnp.float32)
    stream = stream_ref[...]
    moved = moved_ref[...]
    weighted = weighted_ref[...]
    sums = [
        jnp.sum(stream * stream, axis=1, keepdims=True),
        jnp.sum(weighted * stream, axis=1, keepdims=True),
        jnp.sum(weighted * moved, axis=1, keepdims=True),
        jnp.sum(stream * moved, axis=1, keepdims=True),
    ]
    lane = lax.broadcasted_iota(jnp.int32, (2 * HALF, 128), 1)
    table = jnp.zeros((2 * HALF, 128), jnp.float32)
    for i, value in enumerate(sums):
        table = jnp.where(lane == i, value, table)
    turned = table.T
    packed = jnp.concatenate([turned[:4, :HALF], turned[:4, HALF:]], axis=0)
    for i in range(stats_ref.shape[0]):
        stats_ref[i] = packed


def second_kernel(
    ids_ref, stats_ref, stream_ref, moved_ref, weighted_ref,
    n0, n1, n2, n3, f0, f1, f2, f3,
    own_ref, side_ref, even_ref, odd_ref, curv_ref, a_ref, sems,
):
    copies = [
        pltpu.make_async_copy(piece, a_ref.at[pl.ds(i * PIECE, PIECE)], sems.at[i])
        for i, piece in enumerate((n0, n1, n2, n3, f0, f1, f2, f3))
    ]
    for copy in copies:
        copy.start()
    total = jnp.sum(stats_ref[...], axis=0)
    coefs = []
    for h in range(2):
        sum_sq, along_c, tangent_c, cross = (
            total[4 * h + i : 4 * h + i + 1] for i in range(4)
        )
        inv = lax.rsqrt(sum_sq / D + EPS)
        inv3 = inv * inv * inv
        inv5 = inv3 * inv * inv
        share = cross / D
        coefs.append(-inv3 * share)
        coefs.append((3.0 * inv5 * share * along_c - inv3 * tangent_c) / D)
        coefs.append(-inv3 * along_c / D)
    coefs.append(jnp.zeros((128 - len(coefs), HALF), jnp.float32))
    turned = jnp.concatenate(coefs, axis=0).T
    for h in range(2):
        rows = pl.ds(h * HALF, HALF)
        curv_ref[rows, :] = (
            turned[:, 3 * h : 3 * h + 1] * weighted_ref[rows, :]
            + turned[:, 3 * h + 1 : 3 * h + 2] * stream_ref[rows, :]
            + turned[:, 3 * h + 2 : 3 * h + 3] * moved_ref[rows, :]
        )
    me = ids_ref[0]
    core = me % NC
    colors = piece_colors(me)
    curv = jnp.concatenate(
        [curv_ref[piece_rows(core * HALF, q), :] for q in colors]
        + [curv_ref[piece_rows((1 - core) * HALF, q), :] for q in colors],
        axis=0,
    )
    curv_t = curv.T.astype(jnp.bfloat16)
    for copy in copies:
        copy.wait()
    color = ids_ref[1]
    to_even = 1 + 2 * (color % 2)
    for out_ref, step in (
        (side_ref, 2), (even_ref, to_even), (odd_ref, 4 - to_even), (own_ref, 0)
    ):
        q = (color + step) % 4
        for pair in range(4):
            z = 2 * pair + q % 2
            h = ((z - q + 8) % 4) // 2
            columns = []
            for k in range(2):
                at = pl.ds(pl.multiple_of((z * NH + h + 2 * k) * 128, 128), 128)
                columns.append(a_ref[:, at])
            out = jnp.dot(
                curv_t,
                jnp.concatenate(columns, axis=1),
                preferred_element_type=jnp.float32,
            ).astype(jnp.bfloat16)
            out_ref[2 * pair] = out[:, :128]
            out_ref[2 * pair + 1] = out[:, 128:]


def third_kernel(side_ref, own_ref, even_ref, odd_ref, out_ref):
    f32 = jnp.float32
    for i in range(own_ref.shape[0]):
        out_ref[i] = (
            own_ref[i].astype(f32)
            + even_ref[i].astype(f32)
            + odd_ref[i].astype(f32)
            + side_ref[i].astype(f32)
        ).astype(out_ref.dtype)


def last_kernel(parts_ref, out_ref):
    total = parts_ref[0].astype(jnp.float32)
    for i in range(1, parts_ref.shape[0]):
        total = total + parts_ref[i].astype(jnp.float32)
    out_ref[...] = total.T.astype(out_ref.dtype)


def local(attn_out, residual, out_weight, tangent, norm_gain, cotangent, seq_len):
    f32, bf16 = jnp.float32, jnp.bfloat16
    rows, columns = residual.shape
    features = attn_out.shape[1]
    me = lax.axis_index("fsdp")
    rep = lax.axis_index("rep")
    color = (rep // NH + 2 * (rep % NH)) % 4
    ids = jnp.stack([me, color]).astype(jnp.int32)
    gain = norm_gain[None, :]

    def in_group(x, step):
        return lax.ppermute(x, "fsdp", fsdp_perm(step))

    def of_groups(x, step):
        return lax.ppermute(x, "rep", rep_perm(step))

    def shape(*dims, dtype=f32):
        return jax.ShapeDtypeStruct(dims, dtype)

    own = lax.all_to_all(
        jnp.broadcast_to(attn_out[None], (4, SHARD, features)),
        "fsdp", 0, 0, axis_index_groups=TEAMS,
    ).reshape(PIECE, features)
    near = [
        own,
        in_group(own, lambda x, y, c: (x, even_partner(y), c)),
        in_group(own, lambda x, y, c: (x, odd_partner(y), c)),
        in_group(own, lambda x, y, c: (x + 1, y, c)),
    ]
    ready, gain, ids = lax.optimization_barrier((own, gain, ids))
    far = [in_group(piece, lambda x, y, c: (x, y, c + 1)) for piece in [ready] + near[1:]]

    near_s = pl.pallas_call(
        near_kernel,
        out_shape=shape(HALF, columns),
        in_specs=[VMEM] * 5,
        out_specs=VMEM,
        compiler_params=PARAMS,
        name="near",
    )(*near, out_weight)

    whole = shape(rows, columns)
    stream, moved, weighted, stats = pl.pallas_call(
        far_kernel,
        out_shape=(whole, whole, whole, shape(32, 8, HALF)),
        in_specs=[SMEM, SMEM] + [VMEM] * 14,
        out_specs=(VMEM,) * 4,
        compiler_params=PARAMS,
        name="far",
    )(
        ids, seq_len, *near, *far, out_weight, tangent, near_s,
        residual, cotangent, gain,
    )

    stats = lax.all_to_all(stats, "fsdp", 0, 0)

    whole = shape(8, columns, 128, dtype=bf16)
    mine, side, even, odd = pl.pallas_call(
        second_kernel,
        out_shape=(whole,) * 4,
        in_specs=[SMEM] + [VMEM] * 4 + [ANY] * 8,
        out_specs=(VMEM,) * 4,
        scratch_shapes=[
            pltpu.VMEM((rows, columns), f32),
            pltpu.VMEM((rows, features), bf16),
            pltpu.SemaphoreType.DMA((8,)),
        ],
        compiler_params=PARAMS,
        name="second",
    )(ids, stats, stream, moved, weighted, *near, *far)

    side = lax.ppermute(side, ("rep", "fsdp"), side_perm())
    even = of_groups(even, lambda z, h: (even_partner(z), h))
    odd = of_groups(odd, lambda z, h: (odd_partner(z), h))
    four = pl.pallas_call(
        third_kernel,
        out_shape=whole,
        in_specs=[VMEM] * 4,
        out_specs=VMEM,
        compiler_params=PARAMS,
        name="third",
    )(side, mine, even, odd)
    parts = lax.all_to_all(four, "rep", 0, 0, axis_index_groups=CLASSES)
    return pl.pallas_call(
        last_kernel,
        out_shape=shape(128, columns, dtype=bf16),
        in_specs=[VMEM],
        out_specs=VMEM,
        compiler_params=PARAMS,
        name="last",
    )(parts)


def solution(mesh):
    in_specs = (
        P(("rep", "fsdp"), None),
        P("rep", "fsdp"),
        P(None, "fsdp"),
        P(None, "fsdp"),
        P("fsdp"),
        P("rep", "fsdp"),
        P("rep"),
    )
    out_specs = P("rep", "fsdp")
    return jax.shard_map(local, mesh=mesh, in_specs=in_specs, out_specs=out_specs, check_vma=False)
```

```python
import jax
import jax.numpy as jnp
from jax import lax
from jax.experimental import pallas as pl
from jax.experimental.pallas import tpu as pltpu
from jax.sharding import PartitionSpec as P

D = 8192
EPS = 1e-05
NX, NY, NC = 2, 8, 2
NZ, NH = 8, 4
SHARD = 16
PIECE = 64
HALF = 256
VMEM = pl.BlockSpec(memory_space=pltpu.VMEM)
SMEM = pl.BlockSpec(memory_space=pltpu.SMEM)
PARAMS = pltpu.CompilerParams(vmem_limit_bytes=16 * 1024 * 1024)


def fsdp_of(x, y, c):
    return (x % NX * NY + y % NY) * NC + c % NC


def fsdp_perm(step):
    return [
        (fsdp_of(x, y, c), fsdp_of(*step(x, y, c)))
        for x in range(NX)
        for y in range(NY)
        for c in range(NC)
    ]


def rep_of(z, h):
    return z % NZ * NH + h % NH


def rep_perm(step):
    return [(rep_of(z, h), rep_of(*step(z, h))) for z in range(NZ) for h in range(NH)]


def even_partner(i):
    return i ^ 1


def odd_partner(i):
    return ((i + 1) ^ 1) - 1


def side_perm():
    moves = []
    for z in range(NZ):
        for h in range(NH):
            for f in range(NX * NY * NC):
                there = odd_partner(h) if f % NC else even_partner(h)
                width = NX * NY * NC
                moves.append((rep_of(z, h) * width + f, rep_of(z, there) * width + f))
    return moves


def chip_of(q, j):
    x = j // 2
    return x, (q + 2 * x) % 4 + 4 * (j % 2)


TEAMS = [[fsdp_of(*chip_of(q, j), c) for j in range(4)] for q in range(4) for c in range(NC)]
CLASSES = [
    [rep_of(z, h) for z in range(NZ) for h in range(NH) if (z + 2 * h) % 4 == q]
    for q in range(4)
]
BLOCKS = [fsdp_of(*chip_of(q, j), c) for c in range(NC) for q in range(4) for j in range(4)]


def piece_colors(me):
    x, y = me // (NY * NC), (me // NC) % NY
    own = (y + 2 * x) % 4
    to_even = 1 + 2 * (y % 2)
    return [own, (own + to_even) % 4, (own + 4 - to_even) % 4, (own + 2) % 4]


def piece_rows(first, color):
    return pl.ds(pl.multiple_of(first + color * PIECE, PIECE), PIECE)


def product(pieces, w_ref):
    a = jnp.concatenate([piece[...] for piece in pieces], axis=0)
    return jnp.dot(a, w_ref[...], preferred_element_type=jnp.float32)


def near_kernel(p0, p1, p2, p3, w_ref, s_ref):
    s_ref[...] = product((p0, p1, p2, p3), w_ref)


def far_kernel(
    me_ref, len_ref, n0, n1, n2, n3, f0, f1, f2, f3, w_ref, t_ref, near_s_ref,
    res_ref, cot_ref, gain_ref,
    stream_ref, moved_ref, weighted_ref, stats_ref,
):
    me = me_ref[0]
    core = me % NC
    near, far = (n0, n1, n2, n3), (f0, f1, f2, f3)
    for first, target, value in (
        (core, stream_ref, near_s_ref[...]),
        (1 - core, stream_ref, product(far, w_ref)),
        (core, moved_ref, product(near, t_ref)),
        (1 - core, moved_ref, product(far, t_ref)),
    ):
        for i, color in enumerate(piece_colors(me)):
            target[piece_rows(first * HALF, color), :] = value[i * PIECE : (i + 1) * PIECE]
    gain = gain_ref[...].astype(jnp.float32)
    for i, block in enumerate(BLOCKS):
        token = block * SHARD + lax.broadcasted_iota(jnp.int32, (SHARD, 1), 0)
        live = (token < len_ref[0]).astype(jnp.float32)
        there = pl.ds(i * SHARD, SHARD)
        here = pl.ds(block * SHARD, SHARD)
        weighted_ref[there, :] = cot_ref[here, :].astype(jnp.float32) * gain * live
        stream_ref[there, :] += res_ref[here, :].astype(jnp.float32)
    stream = stream_ref[...]
    moved = moved_ref[...]
    weighted = weighted_ref[...]
    sums = [
        jnp.sum(stream * stream, axis=1, keepdims=True),
        jnp.sum(weighted * stream, axis=1, keepdims=True),
        jnp.sum(weighted * moved, axis=1, keepdims=True),
        jnp.sum(stream * moved, axis=1, keepdims=True),
    ]
    lane = lax.broadcasted_iota(jnp.int32, (2 * HALF, 128), 1)
    table = jnp.zeros((2 * HALF, 128), jnp.float32)
    for i, value in enumerate(sums):
        table = jnp.where(lane == i, value, table)
    turned = table.T
    packed = jnp.concatenate([turned[:4, :HALF], turned[:4, HALF:]], axis=0)
    for i in range(stats_ref.shape[0]):
        stats_ref[i] = packed


def second_kernel(
    ids_ref, stats_ref, stream_ref, moved_ref, weighted_ref,
    n0, n1, n2, n3, f0, f1, f2, f3,
    own_ref, side_ref, even_ref, odd_ref, curv_ref,
):
    total = jnp.sum(stats_ref[...], axis=0)
    coefs = []
    for h in range(2):
        sum_sq, along_c, tangent_c, cross = (
            total[4 * h + i : 4 * h + i + 1] for i in range(4)
        )
        inv = lax.rsqrt(sum_sq / D + EPS)
        inv3 = inv * inv * inv
        inv5 = inv3 * inv * inv
        share = cross / D
        coefs.append(-inv3 * share)
        coefs.append((3.0 * inv5 * share * along_c - inv3 * tangent_c) / D)
        coefs.append(-inv3 * along_c / D)
    coefs.append(jnp.zeros((128 - len(coefs), HALF), jnp.float32))
    turned = jnp.concatenate(coefs, axis=0).T
    for h in range(2):
        rows = pl.ds(h * HALF, HALF)
        curv_ref[rows, :] = (
            turned[:, 3 * h : 3 * h + 1] * weighted_ref[rows, :]
            + turned[:, 3 * h + 1 : 3 * h + 2] * stream_ref[rows, :]
            + turned[:, 3 * h + 2 : 3 * h + 3] * moved_ref[rows, :]
        )
    me = ids_ref[0]
    core = me % NC
    colors = piece_colors(me)
    curv = jnp.concatenate(
        [curv_ref[piece_rows(core * HALF, q), :] for q in colors]
        + [curv_ref[piece_rows((1 - core) * HALF, q), :] for q in colors],
        axis=0,
    )
    curv_t = curv.T.astype(jnp.bfloat16)
    pieces = (n0, n1, n2, n3, f0, f1, f2, f3)
    color = ids_ref[1]
    to_even = 1 + 2 * (color % 2)
    for out_ref, step in (
        (side_ref, 2), (even_ref, to_even), (odd_ref, 4 - to_even), (own_ref, 0)
    ):
        q = (color + step) % 4
        for pair in range(4):
            z = 2 * pair + q % 2
            h = ((z - q + 8) % 4) // 2
            columns = []
            for k in range(2):
                at = pl.ds(pl.multiple_of((z * NH + h + 2 * k) * 128, 128), 128)
                columns.append(jnp.concatenate([p[:, at] for p in pieces], axis=0))
            out = jnp.dot(
                curv_t,
                jnp.concatenate(columns, axis=1),
                preferred_element_type=jnp.float32,
            ).astype(jnp.bfloat16)
            out_ref[2 * pair] = out[:, :128]
            out_ref[2 * pair + 1] = out[:, 128:]


def third_kernel(side_ref, own_ref, even_ref, odd_ref, out_ref):
    f32 = jnp.float32
    for i in range(own_ref.shape[0]):
        out_ref[i] = (
            own_ref[i].astype(f32)
            + even_ref[i].astype(f32)
            + odd_ref[i].astype(f32)
            + side_ref[i].astype(f32)
        ).astype(out_ref.dtype)


def last_kernel(parts_ref, out_ref):
    total = parts_ref[0].astype(jnp.float32)
    for i in range(1, parts_ref.shape[0]):
        total = total + parts_ref[i].astype(jnp.float32)
    out_ref[...] = total.T.astype(out_ref.dtype)


def local(attn_out, residual, out_weight, tangent, norm_gain, cotangent, seq_len):
    f32, bf16 = jnp.float32, jnp.bfloat16
    rows, columns = residual.shape
    features = attn_out.shape[1]
    me = lax.axis_index("fsdp")
    rep = lax.axis_index("rep")
    color = (rep // NH + 2 * (rep % NH)) % 4
    ids = jnp.stack([me, color]).astype(jnp.int32)
    gain = norm_gain[None, :]

    def in_group(x, step):
        return lax.ppermute(x, "fsdp", fsdp_perm(step))

    def of_groups(x, step):
        return lax.ppermute(x, "rep", rep_perm(step))

    def shape(*dims, dtype=f32):
        return jax.ShapeDtypeStruct(dims, dtype)

    own = lax.all_to_all(
        jnp.broadcast_to(attn_out[None], (4, SHARD, features)),
        "fsdp", 0, 0, axis_index_groups=TEAMS,
    ).reshape(PIECE, features)
    near = [
        own,
        in_group(own, lambda x, y, c: (x, even_partner(y), c)),
        in_group(own, lambda x, y, c: (x, odd_partner(y), c)),
        in_group(own, lambda x, y, c: (x + 1, y, c)),
    ]
    ready, gain, ids = lax.optimization_barrier((own, gain, ids))
    far = [in_group(piece, lambda x, y, c: (x, y, c + 1)) for piece in [ready] + near[1:]]

    near_s = pl.pallas_call(
        near_kernel,
        out_shape=shape(HALF, columns),
        in_specs=[VMEM] * 5,
        out_specs=VMEM,
        compiler_params=PARAMS,
        name="near",
    )(*near, out_weight)

    whole = shape(rows, columns)
    stream, moved, weighted, stats = pl.pallas_call(
        far_kernel,
        out_shape=(whole, whole, whole, shape(32, 8, HALF)),
        in_specs=[SMEM, SMEM] + [VMEM] * 14,
        out_specs=(VMEM,) * 4,
        compiler_params=PARAMS,
        name="far",
    )(
        ids, seq_len, *near, *far, out_weight, tangent, near_s,
        residual, cotangent, gain,
    )

    stats = lax.all_to_all(stats, "fsdp", 0, 0)

    whole = shape(8, columns, 128, dtype=bf16)
    mine, side, even, odd = pl.pallas_call(
        second_kernel,
        out_shape=(whole,) * 4,
        in_specs=[SMEM] + [VMEM] * 12,
        out_specs=(VMEM,) * 4,
        scratch_shapes=[pltpu.VMEM((rows, columns), f32)],
        compiler_params=PARAMS,
        name="second",
    )(ids, stats, stream, moved, weighted, *near, *far)

    side = lax.ppermute(side, ("rep", "fsdp"), side_perm())
    even = of_groups(even, lambda z, h: (even_partner(z), h))
    odd = of_groups(odd, lambda z, h: (odd_partner(z), h))
    four = pl.pallas_call(
        third_kernel,
        out_shape=whole,
        in_specs=[VMEM] * 4,
        out_specs=VMEM,
        compiler_params=PARAMS,
        name="third",
    )(side, mine, even, odd)
    parts = lax.all_to_all(four, "rep", 0, 0, axis_index_groups=CLASSES)
    return pl.pallas_call(
        last_kernel,
        out_shape=shape(128, columns, dtype=bf16),
        in_specs=[VMEM],
        out_specs=VMEM,
        compiler_params=PARAMS,
        name="last",
    )(parts)


def solution(mesh):
    in_specs = (
        P(("rep", "fsdp"), None),
        P("rep", "fsdp"),
        P(None, "fsdp"),
        P(None, "fsdp"),
        P("fsdp"),
        P("rep", "fsdp"),
        P("rep"),
    )
    out_specs = P("rep", "fsdp")
    return jax.shard_map(local, mesh=mesh, in_specs=in_specs, out_specs=out_specs, check_vma=False)
```

```python
import jax
import jax.numpy as jnp
from jax import lax
from jax.experimental import pallas as pl
from jax.experimental.pallas import tpu as pltpu
from jax.sharding import PartitionSpec as P

D = 8192
EPS = 1e-05
NX, NY, NC = 2, 8, 2
NZ, NH = 8, 4
SHARD = 16
PIECE = 64
HALF = 256
VMEM = pl.BlockSpec(memory_space=pltpu.VMEM)
SMEM = pl.BlockSpec(memory_space=pltpu.SMEM)
PARAMS = pltpu.CompilerParams(vmem_limit_bytes=16 * 1024 * 1024)


def fsdp_of(x, y, c):
    return (x % NX * NY + y % NY) * NC + c % NC


def fsdp_perm(step):
    return [
        (fsdp_of(x, y, c), fsdp_of(*step(x, y, c)))
        for x in range(NX)
        for y in range(NY)
        for c in range(NC)
    ]


def rep_of(z, h):
    return z % NZ * NH + h % NH


def rep_perm(step):
    return [(rep_of(z, h), rep_of(*step(z, h))) for z in range(NZ) for h in range(NH)]


def even_partner(i):
    return i ^ 1


def odd_partner(i):
    return ((i + 1) ^ 1) - 1


def side_perm():
    moves = []
    for z in range(NZ):
        for h in range(NH):
            for f in range(NX * NY * NC):
                there = odd_partner(h) if f % NC else even_partner(h)
                width = NX * NY * NC
                moves.append((rep_of(z, h) * width + f, rep_of(z, there) * width + f))
    return moves


def chip_of(q, j):
    x = j // 2
    return x, (q + 2 * x) % 4 + 4 * (j % 2)


TEAMS = [[fsdp_of(*chip_of(q, j), c) for j in range(4)] for q in range(4) for c in range(NC)]
CLASSES = [
    [rep_of(z, h) for z in range(NZ) for h in range(NH) if (z + 2 * h) % 4 == q]
    for q in range(4)
]
BLOCKS = [fsdp_of(*chip_of(q, j), c) for c in range(NC) for q in range(4) for j in range(4)]


def piece_colors(me):
    x, y = me // (NY * NC), (me // NC) % NY
    own = (y + 2 * x) % 4
    to_even = 1 + 2 * (y % 2)
    return [own, (own + to_even) % 4, (own + 4 - to_even) % 4, (own + 2) % 4]


def piece_rows(first, color):
    return pl.ds(pl.multiple_of(first + color * PIECE, PIECE), PIECE)


def product(pieces, w_ref):
    a = jnp.concatenate([piece[...] for piece in pieces], axis=0)
    return jnp.dot(a, w_ref[...], preferred_element_type=jnp.float32)


def near_kernel(p0, p1, p2, p3, w_ref, s_ref):
    s_ref[...] = product((p0, p1, p2, p3), w_ref)


def far_kernel(
    me_ref, len_ref, n0, n1, n2, n3, f0, f1, f2, f3, w_ref, t_ref, near_s_ref,
    res_ref, cot_ref, gain_ref,
    stream_ref, moved_ref, weighted_ref, stats_ref,
):
    me = me_ref[0]
    core = me % NC
    near, far = (n0, n1, n2, n3), (f0, f1, f2, f3)
    for first, target, value in (
        (core, stream_ref, near_s_ref[...]),
        (1 - core, stream_ref, product(far, w_ref)),
        (core, moved_ref, product(near, t_ref)),
        (1 - core, moved_ref, product(far, t_ref)),
    ):
        for i, color in enumerate(piece_colors(me)):
            target[piece_rows(first * HALF, color), :] = value[i * PIECE : (i + 1) * PIECE]
    gain = gain_ref[...].astype(jnp.float32)
    for i, block in enumerate(BLOCKS):
        token = block * SHARD + lax.broadcasted_iota(jnp.int32, (SHARD, 1), 0)
        live = (token < len_ref[0]).astype(jnp.float32)
        there = pl.ds(i * SHARD, SHARD)
        here = pl.ds(block * SHARD, SHARD)
        weighted_ref[there, :] = cot_ref[here, :].astype(jnp.float32) * gain * live
        stream_ref[there, :] += res_ref[here, :].astype(jnp.float32)
    stream = stream_ref[...]
    moved = moved_ref[...]
    weighted = weighted_ref[...]
    sums = [
        jnp.sum(stream * stream, axis=1, keepdims=True),
        jnp.sum(weighted * stream, axis=1, keepdims=True),
        jnp.sum(weighted * moved, axis=1, keepdims=True),
        jnp.sum(stream * moved, axis=1, keepdims=True),
    ]
    lane = lax.broadcasted_iota(jnp.int32, (2 * HALF, 128), 1)
    table = jnp.zeros((2 * HALF, 128), jnp.float32)
    for i, value in enumerate(sums):
        table = jnp.where(lane == i, value, table)
    turned = table.T
    packed = jnp.concatenate([turned[:4, :HALF], turned[:4, HALF:]], axis=0)
    for i in range(stats_ref.shape[0]):
        stats_ref[i] = packed


def second_kernel(
    ids_ref, stats_ref, stream_ref, moved_ref, weighted_ref,
    n0, n1, n2, n3, f0, f1, f2, f3,
    own_ref, side_ref, even_ref, odd_ref, curv_ref,
):
    total = jnp.sum(stats_ref[...], axis=0)
    coefs = []
    for h in range(2):
        sum_sq, along_c, tangent_c, cross = (
            total[4 * h + i : 4 * h + i + 1] for i in range(4)
        )
        inv = lax.rsqrt(sum_sq / D + EPS)
        inv3 = inv * inv * inv
        inv5 = inv3 * inv * inv
        share = cross / D
        coefs.append(-inv3 * share)
        coefs.append((3.0 * inv5 * share * along_c - inv3 * tangent_c) / D)
        coefs.append(-inv3 * along_c / D)
    coefs.append(jnp.zeros((128 - len(coefs), HALF), jnp.float32))
    turned = jnp.concatenate(coefs, axis=0).T
    for h in range(2):
        rows = pl.ds(h * HALF, HALF)
        curv_ref[rows, :] = (
            turned[:, 3 * h : 3 * h + 1] * weighted_ref[rows, :]
            + turned[:, 3 * h + 1 : 3 * h + 2] * stream_ref[rows, :]
            + turned[:, 3 * h + 2 : 3 * h + 3] * moved_ref[rows, :]
        )
    me = ids_ref[0]
    core = me % NC
    colors = piece_colors(me)
    curv = jnp.concatenate(
        [curv_ref[piece_rows(core * HALF, q), :] for q in colors]
        + [curv_ref[piece_rows((1 - core) * HALF, q), :] for q in colors],
        axis=0,
    )
    curv_t = curv.T.astype(jnp.bfloat16)
    pieces = (n0, n1, n2, n3, f0, f1, f2, f3)
    color = ids_ref[1]
    to_even = 1 + 2 * (color % 2)
    for out_ref, step in (
        (side_ref, 2), (even_ref, to_even), (odd_ref, 4 - to_even), (own_ref, 0)
    ):
        q = (color + step) % 4
        for pair in range(4):
            z = 2 * pair + q % 2
            h = ((z - q + 8) % 4) // 2
            columns = []
            for k in range(2):
                at = pl.ds(pl.multiple_of((z * NH + h + 2 * k) * 128, 128), 128)
                columns.append(jnp.concatenate([p[:, at] for p in pieces], axis=0))
            out = jnp.dot(
                curv_t,
                jnp.concatenate(columns, axis=1),
                preferred_element_type=jnp.float32,
            ).astype(jnp.bfloat16)
            out_ref[2 * pair] = out[:, :128]
            out_ref[2 * pair + 1] = out[:, 128:]


def third_kernel(side_ref, own_ref, even_ref, odd_ref, out_ref):
    f32 = jnp.float32
    for i in range(own_ref.shape[0]):
        out_ref[i] = (
            own_ref[i].astype(f32)
            + even_ref[i].astype(f32)
            + odd_ref[i].astype(f32)
            + side_ref[i].astype(f32)
        ).astype(out_ref.dtype)


def last_kernel(parts_ref, out_ref):
    total = parts_ref[0].astype(jnp.float32)
    for i in range(1, parts_ref.shape[0]):
        total = total + parts_ref[i].astype(jnp.float32)
    out_ref[...] = total.T.astype(out_ref.dtype)


def local(attn_out, residual, out_weight, tangent, norm_gain, cotangent, seq_len):
    f32, bf16 = jnp.float32, jnp.bfloat16
    rows, columns = residual.shape
    features = attn_out.shape[1]
    me = lax.axis_index("fsdp")
    rep = lax.axis_index("rep")
    color = (rep // NH + 2 * (rep % NH)) % 4
    ids = jnp.stack([me, color]).astype(jnp.int32)
    gain = norm_gain[None, :]

    def in_group(x, step):
        return lax.ppermute(x, "fsdp", fsdp_perm(step))

    def of_groups(x, step):
        return lax.ppermute(x, "rep", rep_perm(step))

    def shape(*dims, dtype=f32):
        return jax.ShapeDtypeStruct(dims, dtype)

    own = lax.all_gather(attn_out, "fsdp", axis=0, tiled=True, axis_index_groups=TEAMS)
    near = [
        own,
        in_group(own, lambda x, y, c: (x, even_partner(y), c)),
        in_group(own, lambda x, y, c: (x, odd_partner(y), c)),
        in_group(own, lambda x, y, c: (x + 1, y, c)),
    ]
    ready, gain, ids = lax.optimization_barrier((own, gain, ids))
    far = [in_group(piece, lambda x, y, c: (x, y, c + 1)) for piece in [ready] + near[1:]]

    near_s = pl.pallas_call(
        near_kernel,
        out_shape=shape(HALF, columns),
        in_specs=[VMEM] * 5,
        out_specs=VMEM,
        compiler_params=PARAMS,
        name="near",
    )(*near, out_weight)

    whole = shape(rows, columns)
    stream, moved, weighted, stats = pl.pallas_call(
        far_kernel,
        out_shape=(whole, whole, whole, shape(32, 8, HALF)),
        in_specs=[SMEM, SMEM] + [VMEM] * 14,
        out_specs=(VMEM,) * 4,
        compiler_params=PARAMS,
        name="far",
    )(
        ids, seq_len, *near, *far, out_weight, tangent, near_s,
        residual, cotangent, gain,
    )

    stats = lax.all_to_all(stats, "fsdp", 0, 0)

    whole = shape(8, columns, 128, dtype=bf16)
    mine, side, even, odd = pl.pallas_call(
        second_kernel,
        out_shape=(whole,) * 4,
        in_specs=[SMEM] + [VMEM] * 12,
        out_specs=(VMEM,) * 4,
        scratch_shapes=[pltpu.VMEM((rows, columns), f32)],
        compiler_params=PARAMS,
        name="second",
    )(ids, stats, stream, moved, weighted, *near, *far)

    side = lax.ppermute(side, ("rep", "fsdp"), side_perm())
    even = of_groups(even, lambda z, h: (even_partner(z), h))
    odd = of_groups(odd, lambda z, h: (odd_partner(z), h))
    four = pl.pallas_call(
        third_kernel,
        out_shape=whole,
        in_specs=[VMEM] * 4,
        out_specs=VMEM,
        compiler_params=PARAMS,
        name="third",
    )(side, mine, even, odd)
    parts = lax.all_to_all(four, "rep", 0, 0, axis_index_groups=CLASSES)
    return pl.pallas_call(
        last_kernel,
        out_shape=shape(128, columns, dtype=bf16),
        in_specs=[VMEM],
        out_specs=VMEM,
        compiler_params=PARAMS,
        name="last",
    )(parts)


def solution(mesh):
    in_specs = (
        P(("rep", "fsdp"), None),
        P("rep", "fsdp"),
        P(None, "fsdp"),
        P(None, "fsdp"),
        P("fsdp"),
        P("rep", "fsdp"),
        P("rep"),
    )
    out_specs = P("rep", "fsdp")
    return jax.shard_map(local, mesh=mesh, in_specs=in_specs, out_specs=out_specs, check_vma=False)
```
